768 devices in a mesh: slab: 96 (over z, x, core), cross: 8 (over y).
Axes of the slice: x: 4, y: 8, z: 12, core: 2. Of those that a mesh axis runs over, the one named last changes fastest.
Arguments:
- fields: bfloat16 [4, 192, 8, 16, 8, 256], P(None, 'slab', None, 'cross'), may hold values from -1.796875 to 1.796875
- sep_factor: float32 [192, 16, 33, 1024], P('slab', 'cross'), may hold values from -0.03125 to 0.03125
- local_factor: float32 [192, 16, 33, 132], P('slab', 'cross'), may hold values from -0.3125 to 0.3125
Outputs:
- conv_rate: float32 [4, 192, 8, 16, 8, 256], P(None, 'slab', None, 'cross')
- pressure: float32 [192, 16, 33], P('slab', 'cross')
The draws below stay inside these ranges and needn't reach their ends.
All inputs are finite; a program needn't handle non-finite values.
Results may differ from the reference program's by a relative error of at most 0.0004.
Values sent between devices are 32-bit elements; how exact they have to be, the bound alone decides.
No kernel may reach another device: no remote copies, remote signals or barrier semaphores. Data moves between devices by JAX's collectives and lax.ppermute only.
A program may use at most 128 MiB of HBM per device.

```python
import jax
import jax.numpy as jnp
import numpy as np
from jax import lax

EX = 2
EY = 2
EZ = 32
NSEP = 1024
NXE = 192
NYE = 16
NVO = 132
N_SLAB = 96
N_CROSS = 8


def steps_of(rng, extent, split, least, high):
    factor_of = 1.0
    for axis_at, shards_of in split:
        draws = jax.random.uniform(jax.random.fold_in(jax.random.fold_in(rng, 6), axis_at), (shards_of,), jnp.float32, least / len(split), high / len(split))
        factor_of = factor_of * jnp.repeat(jnp.exp(draws), extent[axis_at] // shards_of).reshape((-1,) + (1,) * (len(extent) - 1 - axis_at))
    return factor_of


def bell_draw(own_key, extent, spread, bound, shards=(), held_as=jnp.bfloat16):
    values = spread * jax.random.normal(own_key, extent, jnp.float32)
    if shards:
        values = values * steps_of(own_key, extent, shards, -0.22, 0.18)
    return jnp.clip(values, -bound, bound).astype(held_as)


def setup_inputs(seed: int = 0) -> dict:
    keys = jax.random.split(jax.random.key(seed), 4)
    return {
        "fields": bell_draw(keys[0], (4, NXE, 8, NYE, 8, EZ * 8), 0.3, 1.796875, ((1, 96), (3, 8))),
        "sep_factor": bell_draw(keys[1], (NXE, NYE, EZ + 1, NSEP), (42 * NSEP) ** -0.5, 0.03125, ((0, 96), (1, 8)), jnp.float32),
        "local_factor": bell_draw(keys[2], (NXE, NYE, EZ + 1, NVO), (3 * NVO) ** -0.5, 0.3125, ((0, 96), (1, 8)), jnp.float32),
    }


degree = 7
step_size = 0.25


def legendre_values(order, points):
    earlier = points * 0.0 + 1.0
    current = points * 1.0
    for level_index in range(1, order):
        follow = ((2 * level_index + 1) * points * current - level_index * earlier) / (level_index + 1)
        earlier = current
        current = follow
    return current


def tables():
    gll_nodes = np.array([-1.0, -0.8717401485096066, -0.5917001814331423, -0.2092992179024789,
                          0.2092992179024789, 0.5917001814331423, 0.8717401485096066, 1.0])
    at_nodes = legendre_values(degree, gll_nodes)
    weights = 2.0 / (degree * (degree + 1) * at_nodes ** 2)
    points = degree + 1
    derivative = np.zeros((points, points))
    for target in range(points):
        for source in range(points):
            if target != source:
                derivative[target, source] = at_nodes[target] / (at_nodes[source] * (gll_nodes[target] - gll_nodes[source]))
    derivative[0, 0] = -degree * (degree + 1) / 4.0
    derivative[-1, -1] = degree * (degree + 1) / 4.0
    half_nodes = np.array([0.1252334085114689, 0.3678314989981802, 0.5873179542866175,
                           0.7699026741943047, 0.9041172563704749, 0.9815606342467192])
    fine_nodes = np.concatenate([-half_nodes[::-1], half_nodes])
    for newton_step in range(3):
        top_value = legendre_values(12, fine_nodes)
        below_value = legendre_values(11, fine_nodes)
        slope_value = 12.0 * (fine_nodes * top_value - below_value) / (fine_nodes * fine_nodes - 1.0)
        fine_nodes = fine_nodes - top_value / slope_value
    top_value = legendre_values(12, fine_nodes)
    below_value = legendre_values(11, fine_nodes)
    slope_value = 12.0 * (fine_nodes * top_value - below_value) / (fine_nodes * fine_nodes - 1.0)
    fine_weights = 2.0 / ((1.0 - fine_nodes * fine_nodes) * slope_value * slope_value)
    interp = np.ones((12, points))
    for source in range(points):
        for target in range(points):
            if target != source:
                interp[:, source] *= (fine_nodes - gll_nodes[target]) / (gll_nodes[source] - gll_nodes[target])
    slope_interp = interp @ derivative
    vertex_hats = np.stack([(1.0 - gll_nodes) / 2.0, (1.0 + gll_nodes) / 2.0]) * weights[None, :]
    return (jnp.asarray(weights, dtype=jnp.float32), jnp.asarray(derivative, dtype=jnp.float32),
            jnp.asarray(interp, dtype=jnp.float32), jnp.asarray(slope_interp, dtype=jnp.float32),
            jnp.asarray(fine_weights, dtype=jnp.float32), jnp.asarray(vertex_hats, dtype=jnp.float32))


def apply_along(matrix, tensor, which):
    highest = lax.Precision.HIGHEST
    if which == 1:
        return jnp.einsum('pi,fijke->fpjke', matrix, tensor, precision=highest)
    if which == 2:
        return jnp.einsum('pj,fijke->fipke', matrix, tensor, precision=highest)
    return jnp.einsum('pk,fijke->fijpe', matrix, tensor, precision=highest)


def convect(nodes_last, interp, slope_interp, fine_weights):
    along_z = apply_along(interp, nodes_last, 3)
    along_yz = apply_along(interp, along_z, 2)
    velocity = apply_along(interp, along_yz[:3], 1)
    slope_x = apply_along(slope_interp, along_yz, 1)
    slope_y = apply_along(interp, apply_along(slope_interp, along_z, 2), 1)
    slope_z = apply_along(interp, apply_along(interp, apply_along(slope_interp, nodes_last, 3), 2), 1)
    weight_cube = (fine_weights[:, None, None, None] * fine_weights[None, :, None, None]
                   * fine_weights[None, None, :, None])
    product = (velocity[0:1] * slope_x + velocity[1:2] * slope_y + velocity[2:3] * slope_z) * weight_cube
    back = interp.T
    return apply_along(back, apply_along(back, apply_along(back, product, 1), 2), 3)


def assemble_vertical(tensor):
    layout = tensor.shape
    by_element = tensor.reshape(layout[:-1] + (layout[-1] // 8, 8))
    upper_sum = by_element[..., :-1, 7] + by_element[..., 1:, 0]
    lower_edge = jnp.concatenate([by_element[..., :1, 0], upper_sum], axis=-1)
    upper_edge = jnp.concatenate([upper_sum, by_element[..., -1:, 7]], axis=-1)
    by_element = jnp.concatenate([lower_edge[..., None], by_element[..., 1:7], upper_edge[..., None]], axis=-1)
    return by_element.reshape(layout)


def node_mass(weights, ez_count):
    edge_weight = weights[0] + weights[7]
    across = jnp.concatenate([edge_weight[None], weights[1:7], edge_weight[None]])
    vertical = assemble_vertical(jnp.tile(weights, ez_count))
    return across[:, None, None, None] * across[None, None, :, None] * vertical[None, None, None, :]


def fold_periodic(tensor, which_dim):
    lower_part = lax.slice_in_dim(tensor, 0, 7, axis=which_dim + 1)
    upper_part = lax.slice_in_dim(tensor, 7, 8, axis=which_dim + 1)
    start_plane = lax.slice_in_dim(lower_part, 0, 1, axis=which_dim + 1) + jnp.roll(upper_part, 1, axis=which_dim)
    return jnp.concatenate([start_plane, lax.slice_in_dim(lower_part, 1, 7, axis=which_dim + 1)], axis=which_dim + 1)


def unfold_periodic(lattice, which_dim):
    following = jnp.roll(lax.slice_in_dim(lattice, 0, 1, axis=which_dim + 1), -1, axis=which_dim)
    return jnp.concatenate([lattice, following], axis=which_dim + 1)


def divergence(velocity, derivative):
    highest = lax.Precision.HIGHEST
    layout = velocity.shape
    by_element = velocity.reshape(layout[:-1] + (layout[-1] // 8, 8))
    along_x = jnp.einsum('pi,xiyjzk->xpyjzk', derivative, by_element[0], precision=highest)
    along_y = jnp.einsum('pj,xiyjzk->xiypzk', derivative, by_element[1], precision=highest)
    along_z = jnp.einsum('pk,xiyjzk->xiyjzp', derivative, by_element[2], precision=highest)
    return along_x + along_y + along_z


def restrict(diverge, vertex_hats):
    highest = lax.Precision.HIGHEST
    section_one = jnp.einsum('ai,xiyjzk->xayjzk', vertex_hats, diverge, precision=highest)
    section_two = jnp.einsum('bj,xayjzk->xaybzk', vertex_hats, section_one, precision=highest)
    return jnp.einsum('ck,xaybzk->xaybzc', vertex_hats, section_two, precision=highest)


def vertical_vertices(corner):
    zero_plane = jnp.zeros_like(corner[..., :1, 0])
    return (jnp.concatenate([corner[..., 0], zero_plane], axis=-1)
            + jnp.concatenate([zero_plane, corner[..., 1]], axis=-1))


def reference(fields, sep_factor, local_factor):
    weights, derivative, interp, slope_interp, fine_weights, vertex_hats = tables()
    highest = lax.Precision.HIGHEST
    nodal_values = fields.astype(jnp.float32)
    slab_rows = jnp.moveaxis(nodal_values, 1, 0)

    def one_row(slab_row):
        nodes_last = slab_row.reshape(4, 8, NYE, 8, EZ, 8).transpose(0, 1, 3, 5, 2, 4)
        nodes_last = nodes_last.reshape(4, 8, 8, 8, NYE * EZ)
        terms = convect(nodes_last, interp, slope_interp, fine_weights)
        terms = terms.reshape(4, 8, 8, 8, NYE, EZ).transpose(0, 1, 4, 2, 5, 3)
        return terms.reshape(4, 8, NYE, 8, EZ * 8)

    raw_terms = jnp.moveaxis(lax.map(one_row, slab_rows), 0, 1)
    lattice = fold_periodic(fold_periodic(raw_terms, 1), 3)
    summed = unfold_periodic(unfold_periodic(lattice, 3), 1)
    summed = assemble_vertical(summed)
    conv_rate = -summed / node_mass(weights, EZ)

    velocity_star = nodal_values[:3] + step_size * conv_rate[:3]
    diverge = divergence(velocity_star, derivative)
    corner = restrict(diverge, vertex_hats)
    stacked = vertical_vertices(corner)
    along_y = stacked[:, :, :, 0] + jnp.roll(stacked[:, :, :, 1], 1, axis=2)
    coarse_rhs = along_y[:, 0] + jnp.roll(along_y[:, 1], 1, axis=0)

    separated = jnp.einsum('xyz,xyzs->s', coarse_rhs, sep_factor, precision=highest)
    blocks_rhs = coarse_rhs.reshape(N_SLAB, EX, N_CROSS, EY, EZ + 1).transpose(0, 2, 1, 3, 4)
    blocks_rhs = blocks_rhs.reshape(N_SLAB * N_CROSS, NVO)
    blocks_local = local_factor.reshape(N_SLAB, EX, N_CROSS, EY, EZ + 1, NVO).transpose(0, 2, 1, 3, 4, 5)
    blocks_local = blocks_local.reshape(N_SLAB * N_CROSS, NVO, NVO)
    inner_part = jnp.einsum('dv,dvc->dc', blocks_rhs, blocks_local, precision=highest)
    local_term = jnp.einsum('dvc,dc->dv', blocks_local, inner_part, precision=highest)
    local_term = local_term.reshape(N_SLAB, N_CROSS, EX, EY, EZ + 1).transpose(0, 2, 1, 3, 4)
    local_term = local_term.reshape(NXE, NYE, EZ + 1)
    pressure = jnp.einsum('xyzs,s->xyz', sep_factor, separated, precision=highest) + local_term
    return conv_rate, pressure
```

```python
import functools

import jax
import jax.numpy as jnp
import numpy as np
from jax import lax
from jax.experimental import pallas as pl
from jax.experimental.pallas import tpu as pltpu
from jax.sharding import Mesh
from jax.sharding import PartitionSpec as P

degree = 7
step_size = 0.25
bf16 = jnp.bfloat16
f32 = jnp.float32


def legendre_values(order, points):
    earlier = points * 0.0 + 1.0
    current = points * 1.0
    for level_index in range(1, order):
        follow = ((2 * level_index + 1) * points * current - level_index * earlier) / (
            level_index + 1
        )
        earlier = current
        current = follow
    return current


def tables():
    gll_nodes = np.array(
        [
            -1.0,
            -0.8717401485096066,
            -0.5917001814331423,
            -0.2092992179024789,
            0.2092992179024789,
            0.5917001814331423,
            0.8717401485096066,
            1.0,
        ]
    )
    at_nodes = legendre_values(degree, gll_nodes)
    weights = 2.0 / (degree * (degree + 1) * at_nodes**2)
    points = degree + 1
    derivative = np.zeros((points, points))
    for target in range(points):
        for source in range(points):
            if target != source:
                derivative[target, source] = at_nodes[target] / (
                    at_nodes[source] * (gll_nodes[target] - gll_nodes[source])
                )
    derivative[0, 0] = -degree * (degree + 1) / 4.0
    derivative[-1, -1] = degree * (degree + 1) / 4.0
    half_nodes = np.array(
        [
            0.1252334085114689,
            0.3678314989981802,
            0.5873179542866175,
            0.7699026741943047,
            0.9041172563704749,
            0.9815606342467192,
        ]
    )
    fine_nodes = np.concatenate([-half_nodes[::-1], half_nodes])
    for newton_step in range(3):
        top_value = legendre_values(12, fine_nodes)
        below_value = legendre_values(11, fine_nodes)
        slope_value = (
            12.0 * (fine_nodes * top_value - below_value) / (fine_nodes * fine_nodes - 1.0)
        )
        fine_nodes = fine_nodes - top_value / slope_value
    top_value = legendre_values(12, fine_nodes)
    below_value = legendre_values(11, fine_nodes)
    slope_value = 12.0 * (fine_nodes * top_value - below_value) / (fine_nodes * fine_nodes - 1.0)
    fine_weights = 2.0 / ((1.0 - fine_nodes * fine_nodes) * slope_value * slope_value)
    interp = np.ones((12, points))
    for source in range(points):
        for target in range(points):
            if target != source:
                interp[:, source] *= (fine_nodes - gll_nodes[target]) / (
                    gll_nodes[source] - gll_nodes[target]
                )
    slope_interp = interp @ derivative
    vertex_hats = np.stack([(1.0 - gll_nodes) / 2.0, (1.0 + gll_nodes) / 2.0]) * weights[None, :]
    return weights, derivative, interp, slope_interp, fine_weights, vertex_hats


def halves(matrix):
    high = matrix.astype(np.float32).astype(jnp.bfloat16)
    low = (matrix - high.astype(np.float64)).astype(np.float32).astype(jnp.bfloat16)
    return high, low


def split(x):
    high = x.astype(bf16)
    return high, (x - high.astype(f32)).astype(bf16)


def constants(ez):
    weights, derivative, interp, slope_interp, fine_weights, hats = tables()
    eye = np.eye(ez)
    spread = np.concatenate([np.kron(eye, interp.T), np.kron(eye, slope_interp.T)], axis=1)
    spread = np.concatenate(halves(spread), axis=0)
    lift = np.concatenate(
        [np.kron(interp, interp), np.kron(slope_interp, interp), np.kron(interp, slope_interp)]
    )
    high, low = halves(lift)
    lift = np.concatenate([high, low, high, low], axis=1)
    across = weights.copy()
    across[0] = across[7] = weights[0] + weights[7]
    back = interp.T * fine_weights[None, :]
    fall = -np.kron(back / across[:, None], back / across[:, None])
    high, low = halves(fall)
    fall = np.concatenate([high, high, low], axis=1)
    joined = np.eye(8 * ez)
    for at in range(ez - 1):
        joined[8 * at + 7, 8 * at + 8] = joined[8 * at + 8, 8 * at + 7] = 1.0
    mass = joined @ np.tile(weights, ez)
    gather = np.kron(eye, back.T) @ joined / mass[None, :]
    high, low = halves(gather)
    gather = np.concatenate([high, high, low], axis=0)
    own, rise = [], []
    slope_hats = hats @ derivative
    for f in range(3):
        own_pair, wide_pair = [], []
        for d in range(2):
            hat = slope_hats if f == d else hats
            rows = 8 if d else 5
            plain = np.zeros((rows, 16))
            for e in range(2):
                for a in range(2):
                    plain[e + a + 1, 8 * e : 8 * e + 8] += hat[a]
            shared = plain.copy()
            for a in range(2):
                shared[a, 0] += hat[a, 7]
                shared[3 + a, 15] += hat[a, 0]
            own_pair.append(plain)
            wide_pair.append(shared)
        own_high, own_low = halves(np.kron(*own_pair))
        wide_high, wide_low = halves(step_size * np.kron(*wide_pair))
        own.append(np.concatenate([own_high, own_low, wide_high, wide_high, wide_low], axis=1))
        hat = slope_hats if f == 2 else hats
        up = np.zeros((8 * ez, 128))
        for e in range(ez):
            for a in range(2):
                up[8 * e : 8 * e + 8, e + a] += hat[a]
        high, low = halves(up)
        rise.append(np.concatenate([high, high, low], axis=0))
    return spread, lift, fall, gather, np.stack(own), np.stack(rise)


def first_kernel(
    fields, spread, lift, fall, gather, own, rise, out, low_x, high_x, low_y, high_y, hold, points, down
):
    nodes = fields[...].astype(f32).reshape(1024, 256).astype(bf16)
    points[...] = jnp.dot(
        jnp.concatenate([nodes, nodes], axis=1), spread[...], preferred_element_type=f32
    ).reshape(points.shape)

    def column(at, carry):
        ex = lax.div(at, 2)
        ey = lax.rem(at, 2)
        speeds = []
        slopes = []
        for f in range(4):
            values = points[f, ex, :, ey].reshape(64, 768)
            high, low = split(values)
            stacked = jnp.concatenate([high, high, low, low], axis=0)
            first = jnp.dot(lift[...], stacked[:, :384], preferred_element_type=f32)
            second = jnp.dot(lift[:144], stacked[:, 384:], preferred_element_type=f32)
            if f < 3:
                speeds.append(first[:144])
            slopes.append((first[144:288], first[288:], second))
        for f in range(4):
            product = sum(speeds[d] * slopes[f][d] for d in range(3))
            high, low = split(product)
            stacked = jnp.concatenate([high, low, high], axis=0)
            fallen = jnp.dot(fall[...], stacked, preferred_element_type=f32)
            down[f, ex, :, ey] = fallen.reshape(8, 8, 384)
        return carry

    lax.fori_loop(0, 4, column, 0)
    high, low = split(down[...].reshape(1024, 384))
    stacked = jnp.concatenate([high, low, high], axis=1)
    out[...] = jnp.dot(stacked, gather[...], preferred_element_type=f32).reshape(out.shape)
    middle = out[:, 0, 7] + out[:, 1, 0]
    out[:, 0, 7] = middle
    out[:, 1, 0] = middle
    middle = out[:, :, :, 0, 7:8] + out[:, :, :, 1, 0:1]
    out[:, :, :, 0, 7:8] = middle
    out[:, :, :, 1, 0:1] = middle
    low_x[:64] = out[:, 0, 0].reshape(64, 256)
    high_x[:64] = out[:, 1, 7].reshape(64, 256)
    low_y[...] = out[:, :, :, 0, 0].reshape(64, 256)
    high_y[...] = out[:, :, :, 1, 7].reshape(64, 256)
    total = jnp.zeros((40, 128), f32)
    for f in range(3):
        high, low = split(out[f].reshape(256, 256))
        part = nodes[256 * f : 256 * (f + 1)]
        stacked = jnp.concatenate([part, part, high, low, high], axis=0)
        flat = jnp.dot(own[f], stacked, preferred_element_type=f32)
        high, low = split(flat)
        total = total + jnp.dot(
            jnp.concatenate([high, low, high], axis=1), rise[f], preferred_element_type=f32
        )
    low_x[64:, :128] = total[:8]
    low_x[64:, 128:] = jnp.zeros((8, 128), f32)
    high_x[64:, :128] = total[24:32]
    high_x[64:, 128:] = total[32:]
    hold[...] = total[8:24]


def second_kernel(from_low, from_high, low_y, high_y, hold, low_out, high_out, hold_out):
    low_out[:64] = low_y[...]
    high_out[:64] = high_y[...]
    for f in range(4):
        first, last = 16 * f, 16 * f + 15
        low_out[first : first + 1] = low_y[first : first + 1] + from_low[first : first + 1]
        low_out[last : last + 1] = low_y[last : last + 1] + from_high[first : first + 1]
        high_out[first : first + 1] = high_y[first : first + 1] + from_low[last : last + 1]
        high_out[last : last + 1] = high_y[last : last + 1] + from_high[last : last + 1]
    near = hold[:8] + from_low[64:, :128]
    far = hold[8:] + from_low[64:, 128:] + from_high[64:, :128]
    hold_out[:8] = near
    hold_out[8:] = far
    low_out[64:, :128] = near
    low_out[64:, 128:] = far
    high_out[64:, :128] = near
    high_out[64:, 128:] = far


def third_kernel(
    partial, low_x, high_x, low_y, high_y, hold, sep, inner, out, sums, term
):
    out[...] = partial[...]
    out[:, 0, 0] = out[:, 0, 0] + low_x[:64].reshape(4, 2, 8, 256)
    out[:, 1, 7] = out[:, 1, 7] + high_x[:64].reshape(4, 2, 8, 256)
    out[:, :, :, 0, 0] = out[:, :, :, 0, 0] + low_y[:64].reshape(4, 2, 8, 256)
    out[:, :, :, 1, 7] = out[:, :, :, 1, 7] + high_y[:64].reshape(4, 2, 8, 256)
    rows = []
    for vx in range(2):
        side = slice(128 * vx, 128 * vx + 128)
        rows.append(hold[8 * vx + 1 : 8 * vx + 2] + low_y[67:68, side])
        rows.append(
            hold[8 * vx + 2 : 8 * vx + 3] + low_y[68:69, side] + high_y[64:65, side]
        )
    upright = jnp.transpose(jnp.concatenate(rows + rows, axis=0))
    columns = [upright[:33, v : v + 1] for v in range(4)]
    for at in range(8):
        lanes = slice(128 * at, 128 * at + 128)
        total = sum(columns[v] * sep[v // 2, v % 2, :, lanes] for v in range(4))
        total = jnp.sum(total, axis=0, keepdims=True)
        sums[at : at + 1] = total
    total = sum(columns[v] * inner[v // 2, v % 2] for v in range(4))
    total = jnp.sum(total, axis=0, keepdims=True)
    for v in range(4):
        term[v // 2, v % 2 : v % 2 + 1] = lax.dot_general(
            total, inner[v // 2, v % 2], (((1,), (1,)), ((), ())),
            precision=lax.Precision.HIGHEST, preferred_element_type=f32,
        )


def last_kernel(arrived, sep, term, out):
    total = jnp.sum(arrived[...], axis=0)
    ones = jnp.ones((1, 128), f32)
    for v in range(4):
        spread_out = sum(
            sep[v // 2, v % 2, :, 128 * at : 128 * at + 128] * total[at : at + 1] for at in range(8)
        )
        out[v // 2, v % 2 : v % 2 + 1] = term[v // 2, v % 2 : v % 2 + 1] + lax.dot_general(
            ones, spread_out, (((1,), (1,)), ((), ())),
            precision=lax.Precision.HIGHEST, preferred_element_type=f32,
        )


def call(kernel, shapes, arrays, scratch=(), **options):
    whole = pl.BlockSpec(memory_space=pltpu.VMEM)
    return pl.pallas_call(
        kernel,
        out_shape=[jax.ShapeDtypeStruct(s, f32) for s in shapes],
        in_specs=[whole] * len(arrays),
        out_specs=[whole] * len(shapes),
        scratch_shapes=[pltpu.VMEM(s, f32) for s in scratch],
        compiler_params=pltpu.CompilerParams(vmem_limit_bytes=48 * 2**20),
        **options,
    )(*arrays)


def first(fields):
    tabs = [jnp.asarray(t) for t in constants(fields.shape[5] // 8)]
    return call(
        first_kernel,
        [fields.shape, (72, 256), (72, 256), (64, 256), (64, 256), (16, 128)],
        [fields] + tabs,
        [(4, 2, 8, 2, 8, 768), (4, 2, 8, 2, 8, 384)],
    )


def shifted(x, axis, by):
    count = lax.axis_size(axis)
    return lax.ppermute(x, axis, [(i, (i + by) % count) for i in range(count)])


slab = ("z", "x", "core")


def scattered(tile, axis):
    count = lax.axis_size(axis)
    return lax.all_to_all(jnp.broadcast_to(tile, (count,) + tile.shape), axis, 0, 0)


def local(fields, sep_factor, local_factor):
    partial, low_x, high_x, low_y, high_y, hold = first(fields)
    from_high = shifted(low_x, slab, -1)
    from_low = shifted(high_x, slab, 1)
    low_y, high_y, hold = call(
        second_kernel, [(72, 256), (72, 256), (16, 128)], [from_low, from_high, low_y, high_y, hold]
    )
    y_high = shifted(low_y, "cross", -1)
    y_low = shifted(high_y, "cross", 1)
    conv_rate, sums, term = call(
        third_kernel,
        [fields.shape, (8, 128), (2, 2, 33)],
        [partial, from_low, from_high, y_low, y_high, hold, sep_factor, local_factor],
    )
    sums = jnp.sum(scattered(sums, ("x", "core")), axis=0)
    sums = jnp.sum(scattered(sums, "cross"), axis=0)
    sums = scattered(sums, "z")
    pressure = call(last_kernel, [(2, 2, 33)], [sums, sep_factor, term])[0]
    return conv_rate, pressure


def solution(mesh):
    fine = Mesh(mesh.devices.reshape(12, 4, 2, 8), ("z", "x", "core", "cross"))
    return jax.shard_map(
        local,
        mesh=fine,
        in_specs=(
            P(None, slab, None, "cross", None, None),
            P(slab, "cross", None, None),
            P(slab, "cross", None, None),
        ),
        out_specs=(P(None, slab, None, "cross", None, None), P(slab, "cross", None)),
        check_vma=False,
    )
```

```python
import functools

import jax
import jax.numpy as jnp
import numpy as np
from jax import lax
from jax.experimental import pallas as pl
from jax.experimental.pallas import tpu as pltpu
from jax.sharding import Mesh
from jax.sharding import PartitionSpec as P

degree = 7
step_size = 0.25
bf16 = jnp.bfloat16
f32 = jnp.float32


def legendre_values(order, points):
    earlier = points * 0.0 + 1.0
    current = points * 1.0
    for level_index in range(1, order):
        follow = ((2 * level_index + 1) * points * current - level_index * earlier) / (
            level_index + 1
        )
        earlier = current
        current = follow
    return current


def tables():
    gll_nodes = np.array(
        [
            -1.0,
            -0.8717401485096066,
            -0.5917001814331423,
            -0.2092992179024789,
            0.2092992179024789,
            0.5917001814331423,
            0.8717401485096066,
            1.0,
        ]
    )
    at_nodes = legendre_values(degree, gll_nodes)
    weights = 2.0 / (degree * (degree + 1) * at_nodes**2)
    points = degree + 1
    derivative = np.zeros((points, points))
    for target in range(points):
        for source in range(points):
            if target != source:
                derivative[target, source] = at_nodes[target] / (
                    at_nodes[source] * (gll_nodes[target] - gll_nodes[source])
                )
    derivative[0, 0] = -degree * (degree + 1) / 4.0
    derivative[-1, -1] = degree * (degree + 1) / 4.0
    half_nodes = np.array(
        [
            0.1252334085114689,
            0.3678314989981802,
            0.5873179542866175,
            0.7699026741943047,
            0.9041172563704749,
            0.9815606342467192,
        ]
    )
    fine_nodes = np.concatenate([-half_nodes[::-1], half_nodes])
    for newton_step in range(3):
        top_value = legendre_values(12, fine_nodes)
        below_value = legendre_values(11, fine_nodes)
        slope_value = (
            12.0 * (fine_nodes * top_value - below_value) / (fine_nodes * fine_nodes - 1.0)
        )
        fine_nodes = fine_nodes - top_value / slope_value
    top_value = legendre_values(12, fine_nodes)
    below_value = legendre_values(11, fine_nodes)
    slope_value = 12.0 * (fine_nodes * top_value - below_value) / (fine_nodes * fine_nodes - 1.0)
    fine_weights = 2.0 / ((1.0 - fine_nodes * fine_nodes) * slope_value * slope_value)
    interp = np.ones((12, points))
    for source in range(points):
        for target in range(points):
            if target != source:
                interp[:, source] *= (fine_nodes - gll_nodes[target]) / (
                    gll_nodes[source] - gll_nodes[target]
                )
    slope_interp = interp @ derivative
    vertex_hats = np.stack([(1.0 - gll_nodes) / 2.0, (1.0 + gll_nodes) / 2.0]) * weights[None, :]
    return weights, derivative, interp, slope_interp, fine_weights, vertex_hats


def halves(matrix):
    high = matrix.astype(np.float32).astype(jnp.bfloat16)
    low = (matrix - high.astype(np.float64)).astype(np.float32).astype(jnp.bfloat16)
    return high, low


def split(x):
    high = x.astype(bf16)
    return high, (x - high.astype(f32)).astype(bf16)


def constants(ez):
    weights, derivative, interp, slope_interp, fine_weights, hats = tables()
    eye = np.eye(ez)
    flat, steep = np.kron(eye, interp.T), np.kron(eye, slope_interp.T)
    spread = []
    for at, rows in ((0, slice(0, 128)), (2, slice(128, 256)), (1, slice(0, 256))):
        lanes = slice(128 * at, 128 * at + 128)
        spread += halves(np.concatenate([flat[rows, lanes], steep[rows, lanes]], axis=1))
    spread = np.concatenate(spread, axis=0)
    lift = np.concatenate(
        [np.kron(interp, interp), np.kron(slope_interp, interp), np.kron(interp, slope_interp)]
    )
    high, low = halves(lift)
    lift = np.concatenate([high, low, high, low], axis=1)
    across = weights.copy()
    across[0] = across[7] = weights[0] + weights[7]
    back = interp.T * fine_weights[None, :]
    fall = -np.kron(back / across[:, None], back / across[:, None])
    high, low = halves(fall)
    fall = np.concatenate([high, high, low], axis=1)
    joined = np.eye(8 * ez)
    for at in range(ez - 1):
        joined[8 * at + 7, 8 * at + 8] = joined[8 * at + 8, 8 * at + 7] = 1.0
    mass = joined @ np.tile(weights, ez)
    gather = np.kron(eye, back.T) @ joined / mass[None, :]
    sides = []
    for at in (0, 128):
        high, low = halves(gather[at : at + 256, at : at + 128])
        sides.append(np.concatenate([high, high, low], axis=0))
    gather = np.stack(sides)
    own, rise = [], []
    slope_hats = hats @ derivative
    for f in range(3):
        own_pair, wide_pair = [], []
        for d in range(2):
            hat = slope_hats if f == d else hats
            rows = 8 if d else 5
            plain = np.zeros((rows, 16))
            for e in range(2):
                for a in range(2):
                    plain[e + a + 1, 8 * e : 8 * e + 8] += hat[a]
            shared = plain.copy()
            for a in range(2):
                shared[a, 0] += hat[a, 7]
                shared[3 + a, 15] += hat[a, 0]
            own_pair.append(plain)
            wide_pair.append(shared)
        own_high, own_low = halves(np.kron(*own_pair))
        wide_high, wide_low = halves(step_size * np.kron(*wide_pair))
        own.append(np.concatenate([own_high, own_low, wide_high, wide_high, wide_low], axis=1))
        hat = slope_hats if f == 2 else hats
        up = np.zeros((8 * ez, 128))
        for e in range(ez):
            for a in range(2):
                up[8 * e : 8 * e + 8, e + a] += hat[a]
        high, low = halves(up)
        rise.append(np.concatenate([high, high, low], axis=0))
    fall = np.pad(fall.astype(np.float32), ((0, 0), (0, 80))).astype(jnp.bfloat16)
    blocks = [spread, lift, fall[:, :256], fall[:, 256:], np.concatenate(list(gather), axis=1)]
    blocks += [np.pad(own[f][:, 256 * c : 256 * c + 256].astype(np.float32), ((0, 8), (0, 0))).astype(jnp.bfloat16)
               for f in range(3) for c in range(5)]
    blocks += [np.concatenate(rise[:2], axis=1), np.concatenate([rise[2], rise[2]], axis=1)]
    return np.concatenate(blocks, axis=0)


def first_kernel(
    fields_far, table_far, out_far, near_side, far_side, low_y, high_y, hold,
    fields, table, points, down, out, arrivals, departure,
):
    ends = (0, 1024, 1584, 2352, 4608)
    loads = [pltpu.make_async_copy(fields_far, fields, arrivals.at[0])]
    for at in range(4):
        rows = pl.ds(ends[at], ends[at + 1] - ends[at])
        loads.append(
            pltpu.make_async_copy(table_far.at[rows], table.at[rows], arrivals.at[at + 1])
        )
    for load in loads:
        load.start()
    loads[0].wait()
    nodes = fields[...].astype(f32).reshape(1024, 256).astype(bf16)
    loads[1].wait()
    for at, piece, rows in (
        (0, nodes[:, :128], slice(0, 256)),
        (512, nodes[:, 128:], slice(256, 512)),
        (256, nodes, slice(512, 1024)),
    ):
        points[..., at : at + 256] = jnp.dot(
            jnp.concatenate([piece, piece], axis=1), table[rows], preferred_element_type=f32
        ).reshape(4, 2, 8, 2, 8, 256)
    loads[2].wait()

    def column(ex, carry):
        lift = table[1024:1456]
        fall = jnp.concatenate([table[1456:1520], table[1520:1584][:, :176]], axis=1)
        speeds = []
        slopes = []
        for f in range(4):
            first = points[f, ex, :, 0].reshape(64, 768)
            second = points[f, ex, :, 1].reshape(64, 768)
            sides = []
            for side in range(2):
                lanes = [slice(at, at + 128) for at in range(128 * side, 768, 256)]
                pieces = [first[:, at] for at in lanes] + [second[:, at] for at in lanes]
                high, low = split(jnp.concatenate(pieces, axis=1))
                sides.append(jnp.concatenate([high, high, low, low], axis=0))
            flat = jnp.dot(lift, sides[0], preferred_element_type=f32)
            steep = jnp.dot(lift[:144], sides[1], preferred_element_type=f32)
            if f < 3:
                speeds.append(flat[:144])
            slopes.append((flat[144:288], flat[288:], steep))
        for f in range(4):
            product = sum(speeds[d] * slopes[f][d] for d in range(3))
            high, low = split(product)
            stacked = jnp.concatenate([high, low, high], axis=0)
            fallen = jnp.dot(fall, stacked, preferred_element_type=f32)
            down[f, ex, :, 0] = fallen[:, :384].reshape(8, 8, 384)
            down[f, ex, :, 1] = fallen[:, 384:].reshape(8, 8, 384)
        return carry

    lax.fori_loop(0, 2, column, 0)
    high, low = split(down[...].reshape(1024, 384))
    loads[3].wait()
    for at in (0, 128):
        lanes = slice(at, at + 256)
        stacked = jnp.concatenate([high[:, lanes], low[:, lanes], high[:, lanes]], axis=1)
        out[..., at : at + 128] = jnp.dot(
            stacked, table[1584:2352, at : at + 128], preferred_element_type=f32
        ).reshape(4, 2, 8, 2, 8, 128)
    middle = out[:, 0, 7] + out[:, 1, 0]
    out[:, 0, 7] = middle
    out[:, 1, 0] = middle
    middle = out[:, :, :, 0, 7:8] + out[:, :, :, 1, 0:1]
    out[:, :, :, 0, 7:8] = middle
    out[:, :, :, 1, 0:1] = middle
    store = pltpu.make_async_copy(out, out_far, departure)
    store.start()
    low_y[...] = out[:, :, :, 0, 0].reshape(64, 256)
    high_y[...] = out[:, :, :, 1, 7].reshape(64, 256)
    loads[4].wait()
    total = jnp.zeros((40, 128), f32)
    for f in range(3):
        high, low = split(out[f].reshape(256, 256))
        part = nodes[256 * f : 256 * (f + 1)]
        stacked = jnp.concatenate([part, part, high, low, high], axis=0)
        own = [table[2352 + 48 * c : 2400 + 48 * c] for c in range(5 * f, 5 * f + 5)]
        flat = jnp.dot(jnp.concatenate(own, axis=1), stacked, preferred_element_type=f32)
        high, low = split(flat[:40])
        start, lanes = 3072 + 768 * (f // 2), slice(128 * (f % 2), 128 * (f % 2) + 128)
        total = total + jnp.dot(
            jnp.concatenate([high, low, high], axis=1),
            table[start : start + 768, lanes],
            preferred_element_type=f32,
        )
    hold[...] = total[8:24]
    even = lax.axis_index("core") == 0
    low_face = out[:, 0, 0].reshape(64, 256)
    high_face = out[:, 1, 7].reshape(64, 256)
    far_side[:64] = jnp.where(even, low_face, high_face)
    far_side[64:, :128] = jnp.where(even, total[:8], total[24:32])
    far_side[64:, 128:] = jnp.where(even, 0.0, total[32:])
    chosen = jnp.where(even, high_face, low_face)
    first = jnp.where(even, total[24:32], total[:8])
    second = jnp.where(even, total[32:], 0.0)
    near_side[:64] = chosen
    near_side[64:, :128] = first
    near_side[64:, 128:] = second
    store.wait()


def sides(near_side, far_side, axis):
    me = lax.axis_index(axis)
    even = me == 0
    beside = near_side[1 - me]
    beyond = far_side[...]
    return jnp.where(even, beyond, beside), jnp.where(even, beside, beyond)


def second_kernel(
    near_side, far_side, low_y, high_y, hold, near_out, far_out, hold_out, from_low, from_high
):
    from_low[...], from_high[...] = sides(near_side, far_side, "core")
    even = lax.axis_index("pair") == 0
    low_face = low_y[...]
    high_face = high_y[...]
    near_out[:64] = jnp.where(even, high_face, low_face)
    far_out[:64] = jnp.where(even, low_face, high_face)
    for f in range(4):
        for at, source, row in ((16 * f, from_low, 16 * f), (16 * f + 15, from_high, 16 * f)):
            place = slice(at, at + 1)
            low_sum = low_y[place] + source[row : row + 1]
            high_sum = high_y[place] + source[row + 15 : row + 16]
            near_out[place] = jnp.where(even, high_sum, low_sum)
            far_out[place] = jnp.where(even, low_sum, high_sum)
    near = hold[:8] + from_low[64:, :128]
    far = hold[8:] + from_low[64:, 128:] + from_high[64:, :128]
    hold_out[:8] = near
    hold_out[8:] = far
    for target in (near_out, far_out):
        target[64:, :128] = near
        target[64:, 128:] = far


def third_kernel(partial, from_low, from_high, out):
    out[...] = partial[...]
    out[:, 0, 0] = partial[:, 0, 0] + from_low[:64].reshape(4, 2, 8, 256)
    out[:, 1, 7] = partial[:, 1, 7] + from_high[:64].reshape(4, 2, 8, 256)


def fourth_kernel(near_side, far_side, hold, sep, inner, sums, term):
    low_rows, high_rows = sides(near_side.at[:, 64:], far_side.at[64:], "pair")
    rows = []
    for vx in range(2):
        lanes = slice(128 * vx, 128 * vx + 128)
        rows.append(hold[8 * vx + 1 : 8 * vx + 2] + low_rows[3:4, lanes])
        rows.append(
            hold[8 * vx + 2 : 8 * vx + 3] + low_rows[4:5, lanes] + high_rows[0:1, lanes]
        )
    upright = jnp.transpose(jnp.concatenate(rows + rows, axis=0))
    columns = [upright[:33, v : v + 1] for v in range(4)]
    for at in range(8):
        lanes = slice(128 * at, 128 * at + 128)
        total = sum(columns[v] * sep[v // 2, v % 2, :, lanes] for v in range(4))
        sums[at : at + 1] = jnp.sum(total, axis=0, keepdims=True)
    total = sum(columns[v] * inner[v // 2, v % 2] for v in range(4))
    total = jnp.sum(total, axis=0, keepdims=True)
    for v in range(4):
        term[v // 2, v % 2 : v % 2 + 1] = lax.dot_general(
            total, inner[v // 2, v % 2], (((1,), (1,)), ((), ())),
            precision=lax.Precision.HIGHEST, preferred_element_type=f32,
        )


def fifth_kernel(partial, near_side, far_side, out):
    low_face, high_face = sides(near_side.at[:, :64], far_side.at[:64], "pair")
    out[...] = partial[...]
    out[:, :, :, 0, 0] = partial[:, :, :, 0, 0] + low_face.reshape(4, 2, 8, 256)
    out[:, :, :, 1, 7] = partial[:, :, :, 1, 7] + high_face.reshape(4, 2, 8, 256)


def spread_kernel(parts, copies):
    total = jnp.sum(parts[...], axis=0)
    copies[...] = jnp.broadcast_to(total[None], copies.shape)


def last_kernel(arrived, sep, term, out):
    total = jnp.sum(arrived[...], axis=0)
    ones = jnp.ones((1, 128), f32)
    for v in range(4):
        spread_out = sum(
            sep[v // 2, v % 2, :, 128 * at : 128 * at + 128] * total[at : at + 1] for at in range(8)
        )
        out[v // 2, v % 2 : v % 2 + 1] = term[v // 2, v % 2 : v % 2 + 1] + lax.dot_general(
            ones, spread_out, (((1,), (1,)), ((), ())),
            precision=lax.Precision.HIGHEST, preferred_element_type=f32,
        )


def call(kernel, shapes, arrays):
    whole = pl.BlockSpec(memory_space=pltpu.VMEM)
    return pl.pallas_call(
        kernel,
        out_shape=[jax.ShapeDtypeStruct(s, f32) for s in shapes],
        in_specs=[whole] * len(arrays),
        out_specs=[whole] * len(shapes),
        compiler_params=pltpu.CompilerParams(vmem_limit_bytes=16 * 2**20),
    )(*arrays)


def first(fields):
    arrays = [fields, jnp.asarray(constants(fields.shape[5] // 8))]
    shapes = [fields.shape, (72, 256), (72, 256), (64, 256), (64, 256), (16, 128)]
    whole = pl.BlockSpec(memory_space=pltpu.VMEM)
    beyond = pl.BlockSpec(memory_space=pltpu.HBM)
    return pl.pallas_call(
        first_kernel,
        out_shape=[jax.ShapeDtypeStruct(s, f32) for s in shapes],
        in_specs=[beyond, beyond],
        out_specs=[beyond] + [whole] * 5,
        scratch_shapes=[pltpu.VMEM(a.shape, a.dtype) for a in arrays]
        + [
            pltpu.VMEM((4, 2, 8, 2, 8, 768), f32),
            pltpu.VMEM((4, 2, 8, 2, 8, 384), f32),
            pltpu.VMEM(fields.shape, f32),
            pltpu.SemaphoreType.DMA((5,)),
            pltpu.SemaphoreType.DMA,
        ],
        compiler_params=pltpu.CompilerParams(vmem_limit_bytes=214 * 2**18),
    )(*arrays)


def moved(x, axis, target):
    return lax.ppermute(x, axis, [(i, target(i)) for i in range(lax.axis_size(axis))])


slab = ("z", "x", "core")
cross = ("half", "pair")


def swapped(x, axis):
    count = lax.axis_size(axis)
    return moved(x, axis, lambda i: (i + (1 if i % 2 else count - 1)) % count)


def scattered(parts, axis):
    copies = call(spread_kernel, [(lax.axis_size(axis),) + parts.shape[1:]], [parts])[0]
    return lax.all_to_all(copies, axis, 0, 0)


def local(fields, sep_factor, local_factor):
    partial, near_side, far_side, low_y, high_y, hold = first(fields)
    far_side = swapped(far_side, slab)
    near_side = lax.all_gather(near_side, "core")
    near_y, far_y, hold, from_low, from_high = call(
        second_kernel,
        [(72, 256), (72, 256), (16, 128), (72, 256), (72, 256)],
        [near_side, far_side, low_y, high_y, hold],
    )
    far_y = swapped(far_y, cross)
    near_y = lax.all_gather(near_y, "pair")
    partial = call(third_kernel, [fields.shape], [partial, from_low, from_high])[0]
    sums, term = call(
        fourth_kernel, [(8, 128), (2, 2, 33)], [near_y, far_y, hold, sep_factor, local_factor]
    )
    conv_rate = call(fifth_kernel, [fields.shape], [partial, near_y, far_y])[0]
    sums = lax.all_gather(sums, "core")
    sums = scattered(sums, ("x",) + cross)
    sums = scattered(sums, "z")
    pressure = call(last_kernel, [(2, 2, 33)], [sums, sep_factor, term])[0]
    return conv_rate, pressure


def solution(mesh):
    fine = Mesh(mesh.devices.reshape(12, 4, 2, 4, 2), slab + cross)
    return jax.shard_map(
        local,
        mesh=fine,
        in_specs=(
            P(None, slab, None, cross, None, None),
            P(slab, cross, None, None),
            P(slab, cross, None, None),
        ),
        out_specs=(P(None, slab, None, cross, None, None), P(slab, cross, None)),
        check_vma=False,
    )
```

```python
import functools

import jax
import jax.numpy as jnp
import numpy as np
from jax import lax
from jax.experimental import pallas as pl
from jax.experimental.pallas import tpu as pltpu
from jax.sharding import Mesh
from jax.sharding import PartitionSpec as P

degree = 7
step_size = 0.25
bf16 = jnp.bfloat16
f32 = jnp.float32


def legendre_values(order, points):
    earlier = points * 0.0 + 1.0
    current = points * 1.0
    for level_index in range(1, order):
        follow = ((2 * level_index + 1) * points * current - level_index * earlier) / (
            level_index + 1
        )
        earlier = current
        current = follow
    return current


def tables():
    gll_nodes = np.array(
        [
            -1.0,
            -0.8717401485096066,
            -0.5917001814331423,
            -0.2092992179024789,
            0.2092992179024789,
            0.5917001814331423,
            0.8717401485096066,
            1.0,
        ]
    )
    at_nodes = legendre_values(degree, gll_nodes)
    weights = 2.0 / (degree * (degree + 1) * at_nodes**2)
    points = degree + 1
    derivative = np.zeros((points, points))
    for target in range(points):
        for source in range(points):
            if target != source:
                derivative[target, source] = at_nodes[target] / (
                    at_nodes[source] * (gll_nodes[target] - gll_nodes[source])
                )
    derivative[0, 0] = -degree * (degree + 1) / 4.0
    derivative[-1, -1] = degree * (degree + 1) / 4.0
    half_nodes = np.array(
        [
            0.1252334085114689,
            0.3678314989981802,
            0.5873179542866175,
            0.7699026741943047,
            0.9041172563704749,
            0.9815606342467192,
        ]
    )
    fine_nodes = np.concatenate([-half_nodes[::-1], half_nodes])
    for newton_step in range(3):
        top_value = legendre_values(12, fine_nodes)
        below_value = legendre_values(11, fine_nodes)
        slope_value = (
            12.0 * (fine_nodes * top_value - below_value) / (fine_nodes * fine_nodes - 1.0)
        )
        fine_nodes = fine_nodes - top_value / slope_value
    top_value = legendre_values(12, fine_nodes)
    below_value = legendre_values(11, fine_nodes)
    slope_value = 12.0 * (fine_nodes * top_value - below_value) / (fine_nodes * fine_nodes - 1.0)
    fine_weights = 2.0 / ((1.0 - fine_nodes * fine_nodes) * slope_value * slope_value)
    interp = np.ones((12, points))
    for source in range(points):
        for target in range(points):
            if target != source:
                interp[:, source] *= (fine_nodes - gll_nodes[target]) / (
                    gll_nodes[source] - gll_nodes[target]
                )
    slope_interp = interp @ derivative
    vertex_hats = np.stack([(1.0 - gll_nodes) / 2.0, (1.0 + gll_nodes) / 2.0]) * weights[None, :]
    return weights, derivative, interp, slope_interp, fine_weights, vertex_hats


def halves(matrix):
    high = matrix.astype(np.float32).astype(jnp.bfloat16)
    low = (matrix - high.astype(np.float64)).astype(np.float32).astype(jnp.bfloat16)
    return high, low


def split(x):
    high = x.astype(bf16)
    return high, (x - high.astype(f32)).astype(bf16)


def constants(ez):
    weights, derivative, interp, slope_interp, fine_weights, hats = tables()
    eye = np.eye(ez)
    flat, steep = np.kron(eye, interp.T), np.kron(eye, slope_interp.T)
    spread = []
    for at, rows in ((0, slice(0, 128)), (2, slice(128, 256)), (1, slice(0, 256))):
        lanes = slice(128 * at, 128 * at + 128)
        spread += halves(np.concatenate([flat[rows, lanes], steep[rows, lanes]], axis=1))
    spread = np.concatenate(spread, axis=0)
    lift = np.concatenate(
        [np.kron(slope_interp, interp), np.kron(interp, slope_interp), np.kron(interp, interp)]
    )
    high, low = halves(lift)
    lift = np.concatenate([high, low, high, low], axis=1)
    across = weights.copy()
    across[0] = across[7] = weights[0] + weights[7]
    back = interp.T * fine_weights[None, :]
    fall = -np.kron(back / across[:, None], back / across[:, None])
    high, low = halves(fall)
    fall = np.concatenate([high, high, low], axis=1)
    joined = np.eye(8 * ez)
    for at in range(ez - 1):
        joined[8 * at + 7, 8 * at + 8] = joined[8 * at + 8, 8 * at + 7] = 1.0
    mass = joined @ np.tile(weights, ez)
    gather = np.kron(eye, back.T) @ joined / mass[None, :]
    high, low = halves(gather)
    gather = np.concatenate([high, high, low], axis=0)
    own, rise = [], []
    slope_hats = hats @ derivative
    for f in range(3):
        own_pair, wide_pair = [], []
        for d in range(2):
            hat = slope_hats if f == d else hats
            rows = 8 if d else 5
            plain = np.zeros((rows, 16))
            for e in range(2):
                for a in range(2):
                    plain[e + a + 1, 8 * e : 8 * e + 8] += hat[a]
            shared = plain.copy()
            for a in range(2):
                shared[a, 0] += hat[a, 7]
                shared[3 + a, 15] += hat[a, 0]
            own_pair.append(plain)
            wide_pair.append(shared)
        own_high, own_low = halves(np.kron(*own_pair))
        wide_high, wide_low = halves(step_size * np.kron(*wide_pair))
        own.append(np.concatenate([own_high, own_low, wide_high, wide_high, wide_low], axis=1))
        hat = slope_hats if f == 2 else hats
        up = np.zeros((8 * ez, 128))
        for e in range(ez):
            for a in range(2):
                up[8 * e : 8 * e + 8, e + a] += hat[a]
        high, low = halves(up)
        rise.append(np.concatenate([high, high, low], axis=0))
    fall = np.pad(fall.astype(np.float32), ((0, 0), (0, 80))).astype(jnp.bfloat16)
    blocks = [spread, lift, fall[:, :256], fall[:, 256:], gather]
    blocks += [np.pad(own[f][:, 256 * c : 256 * c + 256].astype(np.float32), ((0, 8), (0, 0))).astype(jnp.bfloat16)
               for f in range(3) for c in range(5)]
    blocks += [np.concatenate(rise[:2], axis=1), np.concatenate([rise[2], rise[2]], axis=1)]
    return np.concatenate(blocks, axis=0)


def first_kernel(
    fields_far, table_far, out_far, near_side, far_side, low_y, high_y, hold,
    fields, table, points, down, out, arrivals, departure,
):
    ends = (0, 1024, 1584, 2736, 4992)
    loads = [pltpu.make_async_copy(fields_far, fields, arrivals.at[0])]
    for at in range(4):
        rows = pl.ds(ends[at], ends[at + 1] - ends[at])
        loads.append(
            pltpu.make_async_copy(table_far.at[rows], table.at[rows], arrivals.at[at + 1])
        )
    for load in loads:
        load.start()
    loads[0].wait()
    nodes = fields[...].astype(f32).reshape(1024, 256).astype(bf16)
    loads[1].wait()
    for at, piece, rows in (
        (0, nodes[:, :128], slice(0, 256)),
        (512, nodes[:, 128:], slice(256, 512)),
        (256, nodes, slice(512, 1024)),
    ):
        points[..., at : at + 256] = jnp.dot(
            jnp.concatenate([piece, piece], axis=1), table[rows], preferred_element_type=f32
        ).reshape(4, 2, 8, 2, 8, 256)
    loads[2].wait()

    def column(ex, carry):
        lift = table[1024:1456]
        fall = jnp.concatenate([table[1456:1520], table[1520:1584][:, :176]], axis=1)
        speeds = []
        slopes = []
        for f in range(4):
            first = points[f, ex, :, 0].reshape(64, 768)
            second = points[f, ex, :, 1].reshape(64, 768)
            sides = []
            for side in range(2):
                lanes = [slice(at, at + 128) for at in range(128 * side, 768, 256)]
                pieces = [first[:, at] for at in lanes] + [second[:, at] for at in lanes]
                high, low = split(jnp.concatenate(pieces, axis=1))
                sides.append(jnp.concatenate([high, high, low, low], axis=0))
            flat = jnp.dot(lift if f < 3 else lift[:288], sides[0], preferred_element_type=f32)
            steep = jnp.dot(lift[288:], sides[1], preferred_element_type=f32)
            if f < 3:
                speeds.append(flat[288:])
            slopes.append((flat[:144], flat[144:288], steep))
        for f in range(4):
            product = sum(speeds[d] * slopes[f][d] for d in range(3))
            high, low = split(product)
            stacked = jnp.concatenate([high, low, high], axis=0)
            fallen = jnp.dot(fall, stacked, preferred_element_type=f32)
            down[f, ex, :, 0] = fallen[:, :384].reshape(8, 8, 384)
            down[f, ex, :, 1] = fallen[:, 384:].reshape(8, 8, 384)
        return carry

    column(0, 0)
    column(1, 0)
    high, low = split(down[...].reshape(1024, 384))
    loads[3].wait()
    stacked = jnp.concatenate([high, low, high], axis=1)
    stores = []
    for pair in range(2):
        part = pl.ds(2 * pair, 2)
        out[part] = jnp.dot(
            stacked[512 * pair : 512 * pair + 512], table[1584:2736], preferred_element_type=f32
        ).reshape(2, 2, 8, 2, 8, 256)
        middle = out[part, 0, 7] + out[part, 1, 0]
        out[part, 0, 7] = middle
        out[part, 1, 0] = middle
        middle = out[part, :, :, 0, 7:8] + out[part, :, :, 1, 0:1]
        out[part, :, :, 0, 7:8] = middle
        out[part, :, :, 1, 0:1] = middle
        stores.append(pltpu.make_async_copy(out.at[part], out_far.at[part], departure.at[pair]))
        stores[pair].start()
    low_y[...] = out[:, :, :, 0, 0].reshape(64, 256)
    high_y[...] = out[:, :, :, 1, 7].reshape(64, 256)
    loads[4].wait()
    total = jnp.zeros((40, 128), f32)
    for f in range(3):
        high, low = split(out[f].reshape(256, 256))
        part = nodes[256 * f : 256 * (f + 1)]
        stacked = jnp.concatenate([part, part, high, low, high], axis=0)
        own = [table[2736 + 48 * c : 2784 + 48 * c] for c in range(5 * f, 5 * f + 5)]
        flat = jnp.dot(jnp.concatenate(own, axis=1), stacked, preferred_element_type=f32)
        high, low = split(flat[:40])
        start, lanes = 3456 + 768 * (f // 2), slice(128 * (f % 2), 128 * (f % 2) + 128)
        total = total + jnp.dot(
            jnp.concatenate([high, low, high], axis=1),
            table[start : start + 768, lanes],
            preferred_element_type=f32,
        )
    hold[...] = total[8:24]
    even = lax.axis_index("core") == 0
    low_face = out[:, 0, 0].reshape(64, 256)
    high_face = out[:, 1, 7].reshape(64, 256)
    far_side[:64] = jnp.where(even, low_face, high_face)
    far_side[64:, :128] = jnp.where(even, total[:8], total[24:32])
    far_side[64:, 128:] = jnp.where(even, 0.0, total[32:])
    chosen = jnp.where(even, high_face, low_face)
    first = jnp.where(even, total[24:32], total[:8])
    second = jnp.where(even, total[32:], 0.0)
    near_side[:64] = chosen
    near_side[64:, :128] = first
    near_side[64:, 128:] = second
    for store in stores:
        store.wait()


def sides(near_side, far_side, axis):
    me = lax.axis_index(axis)
    even = me == 0
    beside = near_side[1 - me]
    beyond = far_side[...]
    return jnp.where(even, beyond, beside), jnp.where(even, beside, beyond)


def second_kernel(
    near_side, far_side, low_y, high_y, hold, near_out, far_out, hold_out, from_low, from_high
):
    from_low[...], from_high[...] = sides(near_side, far_side, "core")
    even = lax.axis_index("pair") == 0
    low_face = low_y[...]
    high_face = high_y[...]
    near_out[:64] = jnp.where(even, high_face, low_face)
    far_out[:64] = jnp.where(even, low_face, high_face)
    for f in range(4):
        for at, source, row in ((16 * f, from_low, 16 * f), (16 * f + 15, from_high, 16 * f)):
            place = slice(at, at + 1)
            low_sum = low_y[place] + source[row : row + 1]
            high_sum = high_y[place] + source[row + 15 : row + 16]
            near_out[place] = jnp.where(even, high_sum, low_sum)
            far_out[place] = jnp.where(even, low_sum, high_sum)
    near = hold[:8] + from_low[64:, :128]
    far = hold[8:] + from_low[64:, 128:] + from_high[64:, :128]
    hold_out[:8] = near
    hold_out[8:] = far
    for target in (near_out, far_out):
        target[64:, :128] = near
        target[64:, 128:] = far


def third_kernel(partial, from_low, from_high, out):
    out[...] = partial[...]
    out[:, 0, 0] = partial[:, 0, 0] + from_low[:64].reshape(4, 2, 8, 256)
    out[:, 1, 7] = partial[:, 1, 7] + from_high[:64].reshape(4, 2, 8, 256)


def right_side(near_side, far_side, hold):
    low_rows, high_rows = sides(near_side.at[:, 64:], far_side.at[64:], "pair")
    rows = []
    for vx in range(2):
        lanes = slice(128 * vx, 128 * vx + 128)
        rows.append(hold[8 * vx + 1 : 8 * vx + 2] + low_rows[3:4, lanes])
        rows.append(
            hold[8 * vx + 2 : 8 * vx + 3] + low_rows[4:5, lanes] + high_rows[0:1, lanes]
        )
    upright = jnp.transpose(jnp.concatenate(rows + rows, axis=0))
    return [upright[:33, v : v + 1] for v in range(4)]


def fourth_kernel(near_side, far_side, hold, sep, sums):
    columns = right_side(near_side, far_side, hold)
    for at in range(8):
        lanes = slice(128 * at, 128 * at + 128)
        total = sum(columns[v] * sep[v // 2, v % 2, :, lanes] for v in range(4))
        sums[0, at : at + 1] = jnp.sum(total, axis=0, keepdims=True)
    sums[1:] = jnp.broadcast_to(sums[0][None], (sums.shape[0] - 1, 8, 128))


def inner_kernel(near_side, far_side, hold, inner, term):
    columns = right_side(near_side, far_side, hold)
    total = sum(columns[v] * inner[v // 2, v % 2] for v in range(4))
    total = jnp.sum(total, axis=0, keepdims=True)
    for v in range(4):
        part = inner[v // 2, v % 2] * total
        term[v // 2, v % 2 : v % 2 + 1] = jnp.sum(part, axis=1)[None]


def fifth_kernel(partial, near_side, far_side, out):
    low_face, high_face = sides(near_side.at[:, :64], far_side.at[:64], "pair")
    out[...] = partial[...]
    out[:, :, :, 0, 0] = partial[:, :, :, 0, 0] + low_face.reshape(4, 2, 8, 256)
    out[:, :, :, 1, 7] = partial[:, :, :, 1, 7] + high_face.reshape(4, 2, 8, 256)


def spread_kernel(parts, copies):
    total = jnp.sum(parts[...], axis=0)
    copies[...] = jnp.broadcast_to(total[None], copies.shape)


def last_kernel(arrived, sep, term, out):
    total = jnp.sum(arrived[...], axis=0)
    for v in range(4):
        part = sum(
            sep[v // 2, v % 2, :, 128 * at : 128 * at + 128] * total[at : at + 1] for at in range(8)
        )
        out[v // 2, v % 2 : v % 2 + 1] = (
            term[v // 2, v % 2 : v % 2 + 1] + jnp.sum(part, axis=1)[None]
        )


def call(kernel, shapes, arrays):
    whole = pl.BlockSpec(memory_space=pltpu.VMEM)
    return pl.pallas_call(
        kernel,
        out_shape=[jax.ShapeDtypeStruct(s, f32) for s in shapes],
        in_specs=[whole] * len(arrays),
        out_specs=[whole] * len(shapes),
        compiler_params=pltpu.CompilerParams(vmem_limit_bytes=16 * 2**20),
    )(*arrays)


def first(fields):
    arrays = [fields, jnp.asarray(constants(fields.shape[5] // 8))]
    shapes = [fields.shape, (72, 256), (72, 256), (64, 256), (64, 256), (16, 128)]
    whole = pl.BlockSpec(memory_space=pltpu.VMEM)
    beyond = pl.BlockSpec(memory_space=pltpu.HBM)
    return pl.pallas_call(
        first_kernel,
        out_shape=[jax.ShapeDtypeStruct(s, f32) for s in shapes],
        in_specs=[beyond, beyond],
        out_specs=[beyond] + [whole] * 5,
        scratch_shapes=[pltpu.VMEM(a.shape, a.dtype) for a in arrays]
        + [
            pltpu.VMEM((4, 2, 8, 2, 8, 768), f32),
            pltpu.VMEM((4, 2, 8, 2, 8, 384), f32),
            pltpu.VMEM(fields.shape, f32),
            pltpu.SemaphoreType.DMA((5,)),
            pltpu.SemaphoreType.DMA((2,)),
        ],
        compiler_params=pltpu.CompilerParams(vmem_limit_bytes=214 * 2**18),
    )(*arrays)


def moved(x, axis, target):
    return lax.ppermute(x, axis, [(i, target(i)) for i in range(lax.axis_size(axis))])


slab = ("z", "x", "core")
cross = ("half", "pair")


def swapped(x, axis):
    count = lax.axis_size(axis)
    return moved(x, axis, lambda i: (i + (1 if i % 2 else count - 1)) % count)


def local(fields, sep_factor, local_factor):
    partial, near_side, far_side, low_y, high_y, hold = first(fields)
    far_side = swapped(far_side, slab)
    near_side = lax.all_gather(near_side, "core")
    near_y, far_y, hold, from_low, from_high = call(
        second_kernel,
        [(72, 256), (72, 256), (16, 128), (72, 256), (72, 256)],
        [near_side, far_side, low_y, high_y, hold],
    )
    far_y = swapped(far_y, cross)
    near_y = lax.all_gather(near_y, "pair")
    partial = call(third_kernel, [fields.shape], [partial, from_low, from_high])[0]
    across = ("x",) + cross
    along = ("z", "core")
    sums = call(
        fourth_kernel,
        [(lax.axis_size(across), 8, 128)],
        [near_y, far_y, hold, sep_factor],
    )[0]
    term = call(inner_kernel, [(2, 2, 33)], [near_y, far_y, hold, local_factor])[0]
    conv_rate = call(fifth_kernel, [fields.shape], [partial, near_y, far_y])[0]
    sums = lax.all_to_all(sums, across, 0, 0)
    sums = call(spread_kernel, [(lax.axis_size(along), 8, 128)], [sums])[0]
    sums = lax.all_to_all(sums, along, 0, 0)
    pressure = call(last_kernel, [(2, 2, 33)], [sums, sep_factor, term])[0]
    return conv_rate, pressure


def solution(mesh):
    fine = Mesh(mesh.devices.reshape(12, 4, 2, 4, 2), slab + cross)
    return jax.shard_map(
        local,
        mesh=fine,
        in_specs=(
            P(None, slab, None, cross, None, None),
            P(slab, cross, None, None),
            P(slab, cross, None, None),
        ),
        out_specs=(P(None, slab, None, cross, None, None), P(slab, cross, None)),
        check_vma=False,
    )
```

```python
import functools

import jax
import jax.numpy as jnp
import numpy as np
from jax import lax
from jax.experimental import pallas as pl
from jax.experimental.pallas import tpu as pltpu
from jax.sharding import Mesh
from jax.sharding import PartitionSpec as P

degree = 7
step_size = 0.25
bf16 = jnp.bfloat16
f32 = jnp.float32


def legendre_values(order, points):
    earlier = points * 0.0 + 1.0
    current = points * 1.0
    for level_index in range(1, order):
        follow = ((2 * level_index + 1) * points * current - level_index * earlier) / (
            level_index + 1
        )
        earlier = current
        current = follow
    return current


def tables():
    gll_nodes = np.array(
        [
            -1.0,
            -0.8717401485096066,
            -0.5917001814331423,
            -0.2092992179024789,
            0.2092992179024789,
            0.5917001814331423,
            0.8717401485096066,
            1.0,
        ]
    )
    at_nodes = legendre_values(degree, gll_nodes)
    weights = 2.0 / (degree * (degree + 1) * at_nodes**2)
    points = degree + 1
    derivative = np.zeros((points, points))
    for target in range(points):
        for source in range(points):
            if target != source:
                derivative[target, source] = at_nodes[target] / (
                    at_nodes[source] * (gll_nodes[target] - gll_nodes[source])
                )
    derivative[0, 0] = -degree * (degree + 1) / 4.0
    derivative[-1, -1] = degree * (degree + 1) / 4.0
    half_nodes = np.array(
        [
            0.1252334085114689,
            0.3678314989981802,
            0.5873179542866175,
            0.7699026741943047,
            0.9041172563704749,
            0.9815606342467192,
        ]
    )
    fine_nodes = np.concatenate([-half_nodes[::-1], half_nodes])
    for newton_step in range(3):
        top_value = legendre_values(12, fine_nodes)
        below_value = legendre_values(11, fine_nodes)
        slope_value = (
            12.0 * (fine_nodes * top_value - below_value) / (fine_nodes * fine_nodes - 1.0)
        )
        fine_nodes = fine_nodes - top_value / slope_value
    top_value = legendre_values(12, fine_nodes)
    below_value = legendre_values(11, fine_nodes)
    slope_value = 12.0 * (fine_nodes * top_value - below_value) / (fine_nodes * fine_nodes - 1.0)
    fine_weights = 2.0 / ((1.0 - fine_nodes * fine_nodes) * slope_value * slope_value)
    interp = np.ones((12, points))
    for source in range(points):
        for target in range(points):
            if target != source:
                interp[:, source] *= (fine_nodes - gll_nodes[target]) / (
                    gll_nodes[source] - gll_nodes[target]
                )
    slope_interp = interp @ derivative
    vertex_hats = np.stack([(1.0 - gll_nodes) / 2.0, (1.0 + gll_nodes) / 2.0]) * weights[None, :]
    return weights, derivative, interp, slope_interp, fine_weights, vertex_hats


def halves(matrix):
    high = matrix.astype(np.float32).astype(jnp.bfloat16)
    low = (matrix - high.astype(np.float64)).astype(np.float32).astype(jnp.bfloat16)
    return high, low


def split(x):
    high = x.astype(bf16)
    return high, (x - high.astype(f32)).astype(bf16)


def constants(ez):
    weights, derivative, interp, slope_interp, fine_weights, hats = tables()
    eye = np.eye(ez)
    flat, steep = np.kron(eye, interp.T), np.kron(eye, slope_interp.T)
    spread = []
    for at, rows in ((0, slice(0, 128)), (2, slice(128, 256)), (1, slice(0, 256))):
        lanes = slice(128 * at, 128 * at + 128)
        spread += halves(np.concatenate([flat[rows, lanes], steep[rows, lanes]], axis=1))
    spread = np.concatenate(spread, axis=0)
    lift = np.concatenate(
        [np.kron(slope_interp, interp), np.kron(interp, slope_interp), np.kron(interp, interp)]
    )
    high, low = halves(lift)
    lift = np.concatenate([high, low, high, low], axis=1)
    across = weights.copy()
    across[0] = across[7] = weights[0] + weights[7]
    back = interp.T * fine_weights[None, :]
    fall = -np.kron(back / across[:, None], back / across[:, None])
    high, low = halves(fall)
    fall = np.concatenate([high, high, low], axis=1)
    joined = np.eye(8 * ez)
    for at in range(ez - 1):
        joined[8 * at + 7, 8 * at + 8] = joined[8 * at + 8, 8 * at + 7] = 1.0
    mass = joined @ np.tile(weights, ez)
    gather = np.kron(eye, back.T) @ joined / mass[None, :]
    high, low = halves(gather)
    gather = np.concatenate([high, high, low], axis=0)
    own, rise = [], []
    slope_hats = hats @ derivative
    for f in range(3):
        own_pair, wide_pair = [], []
        for d in range(2):
            hat = slope_hats if f == d else hats
            rows = 8 if d else 5
            plain = np.zeros((rows, 16))
            for e in range(2):
                for a in range(2):
                    plain[e + a + 1, 8 * e : 8 * e + 8] += hat[a]
            shared = plain.copy()
            for a in range(2):
                shared[a, 0] += hat[a, 7]
                shared[3 + a, 15] += hat[a, 0]
            own_pair.append(plain)
            wide_pair.append(shared)
        own_high, own_low = halves(np.kron(*own_pair))
        wide_high, wide_low = halves(step_size * np.kron(*wide_pair))
        own.append(np.concatenate([own_high, own_low, wide_high, wide_high, wide_low], axis=1))
        hat = slope_hats if f == 2 else hats
        up = np.zeros((8 * ez, 128))
        for e in range(ez):
            for a in range(2):
                up[8 * e : 8 * e + 8, e + a] += hat[a]
        high, low = halves(up)
        rise.append(np.concatenate([high, high, low], axis=0))
    fall = np.pad(fall.astype(np.float32), ((0, 0), (0, 80))).astype(jnp.bfloat16)
    blocks = [spread, lift, fall[:, :256], fall[:, 256:], gather]
    blocks += [np.pad(own[f][:, 256 * c : 256 * c + 256].astype(np.float32), ((0, 8), (0, 0))).astype(jnp.bfloat16)
               for f in range(3) for c in range(5)]
    blocks += [np.concatenate(rise[:2], axis=1), np.concatenate([rise[2], rise[2]], axis=1)]
    return np.concatenate(blocks, axis=0)


def first_kernel(
    fields_far, table_far, out_far, near_side, far_side, low_y, high_y, hold,
    fields, table, points, down, out, arrivals, departure,
):
    ends = (0, 1024, 1584, 2736, 4992)
    loads = [pltpu.make_async_copy(fields_far, fields, arrivals.at[0])]
    for at in range(4):
        rows = pl.ds(ends[at], ends[at + 1] - ends[at])
        loads.append(
            pltpu.make_async_copy(table_far.at[rows], table.at[rows], arrivals.at[at + 1])
        )
    for load in loads:
        load.start()
    loads[0].wait()
    nodes = fields[...].astype(f32).reshape(1024, 256).astype(bf16)
    loads[1].wait()
    for at, piece, rows in (
        (0, nodes[:, :128], slice(0, 256)),
        (512, nodes[:, 128:], slice(256, 512)),
        (256, nodes, slice(512, 1024)),
    ):
        points[..., at : at + 256] = jnp.dot(
            jnp.concatenate([piece, piece], axis=1), table[rows], preferred_element_type=f32
        ).reshape(4, 2, 8, 2, 8, 256)
    loads[2].wait()

    def column(ex, carry):
        lift = table[1024:1456]
        fall = jnp.concatenate([table[1456:1520], table[1520:1584][:, :176]], axis=1)
        speeds = []
        slopes = []
        for f in range(4):
            first = points[f, ex, :, 0].reshape(64, 768)
            second = points[f, ex, :, 1].reshape(64, 768)
            sides = []
            for side in range(2):
                lanes = [slice(at, at + 128) for at in range(128 * side, 768, 256)]
                pieces = [first[:, at] for at in lanes] + [second[:, at] for at in lanes]
                high, low = split(jnp.concatenate(pieces, axis=1))
                sides.append(jnp.concatenate([high, high, low, low], axis=0))
            flat = jnp.dot(lift if f < 3 else lift[:288], sides[0], preferred_element_type=f32)
            steep = jnp.dot(lift[288:], sides[1], preferred_element_type=f32)
            if f < 3:
                speeds.append(flat[288:])
            slopes.append((flat[:144], flat[144:288], steep))
        for f in range(4):
            product = sum(speeds[d] * slopes[f][d] for d in range(3))
            high, low = split(product)
            stacked = jnp.concatenate([high, low, high], axis=0)
            fallen = jnp.dot(fall, stacked, preferred_element_type=f32)
            down[f, ex, :, 0] = fallen[:, :384].reshape(8, 8, 384)
            down[f, ex, :, 1] = fallen[:, 384:].reshape(8, 8, 384)
        return carry

    column(0, 0)
    column(1, 0)
    high, low = split(down[...].reshape(1024, 384))
    loads[3].wait()
    stacked = jnp.concatenate([high, low, high], axis=1)
    stores = []
    for pair in range(2):
        part = pl.ds(2 * pair, 2)
        out[part] = jnp.dot(
            stacked[512 * pair : 512 * pair + 512], table[1584:2736], preferred_element_type=f32
        ).reshape(2, 2, 8, 2, 8, 256)
        middle = out[part, 0, 7] + out[part, 1, 0]
        out[part, 0, 7] = middle
        out[part, 1, 0] = middle
        middle = out[part, :, :, 0, 7:8] + out[part, :, :, 1, 0:1]
        out[part, :, :, 0, 7:8] = middle
        out[part, :, :, 1, 0:1] = middle
        stores.append(pltpu.make_async_copy(out.at[part], out_far.at[part], departure.at[pair]))
        stores[pair].start()
    low_y[...] = out[:, :, :, 0, 0].reshape(64, 256)
    high_y[...] = out[:, :, :, 1, 7].reshape(64, 256)
    loads[4].wait()
    total = jnp.zeros((40, 128), f32)
    for f in range(3):
        high, low = split(out[f].reshape(256, 256))
        part = nodes[256 * f : 256 * (f + 1)]
        stacked = jnp.concatenate([part, part, high, low, high], axis=0)
        own = [table[2736 + 48 * c : 2784 + 48 * c] for c in range(5 * f, 5 * f + 5)]
        flat = jnp.dot(jnp.concatenate(own, axis=1), stacked, preferred_element_type=f32)
        high, low = split(flat[:40])
        start, lanes = 3456 + 768 * (f // 2), slice(128 * (f % 2), 128 * (f % 2) + 128)
        total = total + jnp.dot(
            jnp.concatenate([high, low, high], axis=1),
            table[start : start + 768, lanes],
            preferred_element_type=f32,
        )
    hold[...] = total[8:24]
    even = lax.axis_index("core") == 0
    low_face = out[:, 0, 0].reshape(64, 256)
    high_face = out[:, 1, 7].reshape(64, 256)
    far_side[:64] = jnp.where(even, low_face, high_face)
    far_side[64:, :128] = jnp.where(even, total[:8], total[24:32])
    far_side[64:, 128:] = jnp.where(even, 0.0, total[32:])
    chosen = jnp.where(even, high_face, low_face)
    first = jnp.where(even, total[24:32], total[:8])
    second = jnp.where(even, total[32:], 0.0)
    near_side[:64] = chosen
    near_side[64:, :128] = first
    near_side[64:, 128:] = second
    for store in stores:
        store.wait()


def sides(near_side, far_side, axis):
    me = lax.axis_index(axis)
    even = me == 0
    beside = near_side[1 - me]
    beyond = far_side[...]
    return jnp.where(even, beyond, beside), jnp.where(even, beside, beyond)


def second_kernel(
    near_side, far_side, low_y, high_y, hold, sep, near_out, far_out, hold_out, from_low, from_high
):
    from_low[...], from_high[...] = sides(near_side, far_side, "core")
    even = lax.axis_index("pair") == 0
    low_face = low_y[...]
    high_face = high_y[...]
    near_out[:64] = jnp.where(even, high_face, low_face)
    far_out[:64] = jnp.where(even, low_face, high_face)
    for f in range(4):
        for at, source, row in ((16 * f, from_low, 16 * f), (16 * f + 15, from_high, 16 * f)):
            place = slice(at, at + 1)
            low_sum = low_y[place] + source[row : row + 1]
            high_sum = high_y[place] + source[row + 15 : row + 16]
            near_out[place] = jnp.where(even, high_sum, low_sum)
            far_out[place] = jnp.where(even, low_sum, high_sum)
    near = hold[:8] + from_low[64:, :128]
    far = hold[8:] + from_low[64:, 128:] + from_high[64:, :128]
    hold_out[:8] = near
    hold_out[8:] = far
    for target in (near_out, far_out):
        target[64:, :128] = near
        target[64:, 128:] = far


def third_kernel(partial, from_low, from_high, out):
    out[...] = partial[...]
    out[:, 0, 0] = partial[:, 0, 0] + from_low[:64].reshape(4, 2, 8, 256)
    out[:, 1, 7] = partial[:, 1, 7] + from_high[:64].reshape(4, 2, 8, 256)


def right_side(near_side, far_side, hold):
    low_rows, high_rows = sides(near_side.at[:, 64:], far_side.at[64:], "pair")
    rows = []
    for vx in range(2):
        lanes = slice(128 * vx, 128 * vx + 128)
        rows.append(hold[8 * vx + 1 : 8 * vx + 2] + low_rows[3:4, lanes])
        rows.append(
            hold[8 * vx + 2 : 8 * vx + 3] + low_rows[4:5, lanes] + high_rows[0:1, lanes]
        )
    upright = jnp.transpose(jnp.concatenate(rows + rows, axis=0))
    return [upright[:33, v : v + 1] for v in range(4)]


def fourth_kernel(near_side, far_side, hold, sep, sums):
    columns = right_side(near_side, far_side, hold)
    for at in range(8):
        lanes = slice(128 * at, 128 * at + 128)
        total = sum(columns[v] * sep[v // 2, v % 2, :, lanes] for v in range(4))
        sums[0, at : at + 1] = jnp.sum(total, axis=0, keepdims=True)
    sums[1:] = jnp.broadcast_to(sums[0][None], (sums.shape[0] - 1, 8, 128))


def inner_kernel(near_side, far_side, hold, inner, term):
    columns = right_side(near_side, far_side, hold)
    total = sum(columns[v] * inner[v // 2, v % 2] for v in range(4))
    total = jnp.sum(total, axis=0, keepdims=True)
    for v in range(4):
        part = inner[v // 2, v % 2] * total
        term[v // 2, v % 2 : v % 2 + 1] = jnp.sum(part, axis=1)[None]


def fifth_kernel(partial, near_side, far_side, out):
    low_face, high_face = sides(near_side.at[:, :64], far_side.at[:64], "pair")
    out[...] = partial[...]
    out[:, :, :, 0, 0] = partial[:, :, :, 0, 0] + low_face.reshape(4, 2, 8, 256)
    out[:, :, :, 1, 7] = partial[:, :, :, 1, 7] + high_face.reshape(4, 2, 8, 256)


def spread_kernel(parts, copies):
    total = jnp.sum(parts[...], axis=0)
    copies[...] = jnp.broadcast_to(total[None], copies.shape)


def last_kernel(arrived, sep, term, out):
    total = jnp.sum(arrived[...], axis=0)
    for v in range(4):
        part = sum(
            sep[v // 2, v % 2, :, 128 * at : 128 * at + 128] * total[at : at + 1] for at in range(8)
        )
        out[v // 2, v % 2 : v % 2 + 1] = (
            term[v // 2, v % 2 : v % 2 + 1] + jnp.sum(part, axis=1)[None]
        )


def call(kernel, shapes, arrays):
    whole = pl.BlockSpec(memory_space=pltpu.VMEM)
    return pl.pallas_call(
        kernel,
        out_shape=[jax.ShapeDtypeStruct(s, f32) for s in shapes],
        in_specs=[whole] * len(arrays),
        out_specs=[whole] * len(shapes),
        compiler_params=pltpu.CompilerParams(vmem_limit_bytes=16 * 2**20),
    )(*arrays)


def first(fields):
    arrays = [fields, jnp.asarray(constants(fields.shape[5] // 8))]
    shapes = [fields.shape, (72, 256), (72, 256), (64, 256), (64, 256), (16, 128)]
    whole = pl.BlockSpec(memory_space=pltpu.VMEM)
    beyond = pl.BlockSpec(memory_space=pltpu.HBM)
    return pl.pallas_call(
        first_kernel,
        out_shape=[jax.ShapeDtypeStruct(s, f32) for s in shapes],
        in_specs=[beyond, beyond],
        out_specs=[beyond] + [whole] * 5,
        scratch_shapes=[pltpu.VMEM(a.shape, a.dtype) for a in arrays]
        + [
            pltpu.VMEM((4, 2, 8, 2, 8, 768), f32),
            pltpu.VMEM((4, 2, 8, 2, 8, 384), f32),
            pltpu.VMEM(fields.shape, f32),
            pltpu.SemaphoreType.DMA((5,)),
            pltpu.SemaphoreType.DMA((2,)),
        ],
        compiler_params=pltpu.CompilerParams(vmem_limit_bytes=214 * 2**18),
    )(*arrays)


def moved(x, axis, target):
    return lax.ppermute(x, axis, [(i, target(i)) for i in range(lax.axis_size(axis))])


slab = ("z", "x", "core")
cross = ("half", "pair")


def swapped(x, axis):
    count = lax.axis_size(axis)
    return moved(x, axis, lambda i: (i + (1 if i % 2 else count - 1)) % count)


def local(fields, sep_factor, local_factor):
    partial, near_side, far_side, low_y, high_y, hold = first(fields)
    far_side = swapped(far_side, slab)
    near_side = lax.all_gather(near_side, "core")
    near_y, far_y, hold, from_low, from_high = call(
        second_kernel,
        [(72, 256), (72, 256), (16, 128), (72, 256), (72, 256)],
        [near_side, far_side, low_y, high_y, hold, sep_factor],
    )
    far_y = swapped(far_y, cross)
    near_y = lax.all_gather(near_y, "pair")
    partial = call(third_kernel, [fields.shape], [partial, from_low, from_high])[0]
    across = ("x", "pair", "half")
    along = ("core", "z")
    sums = call(
        fourth_kernel,
        [(lax.axis_size(across), 8, 128)],
        [near_y, far_y, hold, sep_factor],
    )[0]
    term = call(inner_kernel, [(2, 2, 33)], [near_y, far_y, hold, local_factor])[0]
    conv_rate = call(fifth_kernel, [fields.shape], [partial, near_y, far_y])[0]
    sums = lax.all_to_all(sums, across, 0, 0)
    sums = call(spread_kernel, [(lax.axis_size(along), 8, 128)], [sums])[0]
    sums = lax.all_to_all(sums, along, 0, 0)
    pressure = call(last_kernel, [(2, 2, 33)], [sums, sep_factor, term])[0]
    return conv_rate, pressure


def solution(mesh):
    fine = Mesh(mesh.devices.reshape(12, 4, 2, 4, 2), slab + cross)
    return jax.shard_map(
        local,
        mesh=fine,
        in_specs=(
            P(None, slab, None, cross, None, None),
            P(slab, cross, None, None),
            P(slab, cross, None, None),
        ),
        out_specs=(P(None, slab, None, cross, None, None), P(slab, cross, None)),
        check_vma=False,
    )
```

```python
import functools

import jax
import jax.numpy as jnp
import numpy as np
from jax import lax
from jax.experimental import pallas as pl
from jax.experimental.pallas import tpu as pltpu
from jax.sharding import Mesh
from jax.sharding import PartitionSpec as P

degree = 7
step_size = 0.25
bf16 = jnp.bfloat16
f32 = jnp.float32


def legendre_values(order, points):
    earlier = points * 0.0 + 1.0
    current = points * 1.0
    for level_index in range(1, order):
        follow = ((2 * level_index + 1) * points * current - level_index * earlier) / (
            level_index + 1
        )
        earlier = current
        current = follow
    return current


def tables():
    gll_nodes = np.array(
        [
            -1.0,
            -0.8717401485096066,
            -0.5917001814331423,
            -0.2092992179024789,
            0.2092992179024789,
            0.5917001814331423,
            0.8717401485096066,
            1.0,
        ]
    )
    at_nodes = legendre_values(degree, gll_nodes)
    weights = 2.0 / (degree * (degree + 1) * at_nodes**2)
    points = degree + 1
    derivative = np.zeros((points, points))
    for target in range(points):
        for source in range(points):
            if target != source:
                derivative[target, source] = at_nodes[target] / (
                    at_nodes[source] * (gll_nodes[target] - gll_nodes[source])
                )
    derivative[0, 0] = -degree * (degree + 1) / 4.0
    derivative[-1, -1] = degree * (degree + 1) / 4.0
    half_nodes = np.array(
        [
            0.1252334085114689,
            0.3678314989981802,
            0.5873179542866175,
            0.7699026741943047,
            0.9041172563704749,
            0.9815606342467192,
        ]
    )
    fine_nodes = np.concatenate([-half_nodes[::-1], half_nodes])
    for newton_step in range(3):
        top_value = legendre_values(12, fine_nodes)
        below_value = legendre_values(11, fine_nodes)
        slope_value = (
            12.0 * (fine_nodes * top_value - below_value) / (fine_nodes * fine_nodes - 1.0)
        )
        fine_nodes = fine_nodes - top_value / slope_value
    top_value = legendre_values(12, fine_nodes)
    below_value = legendre_values(11, fine_nodes)
    slope_value = 12.0 * (fine_nodes * top_value - below_value) / (fine_nodes * fine_nodes - 1.0)
    fine_weights = 2.0 / ((1.0 - fine_nodes * fine_nodes) * slope_value * slope_value)
    interp = np.ones((12, points))
    for source in range(points):
        for target in range(points):
            if target != source:
                interp[:, source] *= (fine_nodes - gll_nodes[target]) / (
                    gll_nodes[source] - gll_nodes[target]
                )
    slope_interp = interp @ derivative
    vertex_hats = np.stack([(1.0 - gll_nodes) / 2.0, (1.0 + gll_nodes) / 2.0]) * weights[None, :]
    return weights, derivative, interp, slope_interp, fine_weights, vertex_hats


def halves(matrix):
    high = matrix.astype(np.float32).astype(jnp.bfloat16)
    low = (matrix - high.astype(np.float64)).astype(np.float32).astype(jnp.bfloat16)
    return high, low


def split(x):
    high = x.astype(bf16)
    return high, (x - high.astype(f32)).astype(bf16)


def constants(ez):
    weights, derivative, interp, slope_interp, fine_weights, hats = tables()
    eye = np.eye(ez)
    flat, steep = np.kron(eye, interp.T), np.kron(eye, slope_interp.T)
    spread = []
    for at, rows in ((0, slice(0, 128)), (2, slice(128, 256)), (1, slice(0, 256))):
        lanes = slice(128 * at, 128 * at + 128)
        spread += halves(np.concatenate([flat[rows, lanes], steep[rows, lanes]], axis=1))
    spread = np.concatenate(spread, axis=0)
    lift = np.concatenate(
        [np.kron(slope_interp, interp), np.kron(interp, slope_interp), np.kron(interp, interp)]
    )
    high, low = halves(lift)
    lift = np.concatenate([high, low, high, low], axis=1)
    across = weights.copy()
    across[0] = across[7] = weights[0] + weights[7]
    back = interp.T * fine_weights[None, :]
    fall = -np.kron(back / across[:, None], back / across[:, None])
    high, low = halves(fall)
    fall = np.concatenate([high, high, low], axis=1)
    joined = np.eye(8 * ez)
    for at in range(ez - 1):
        joined[8 * at + 7, 8 * at + 8] = joined[8 * at + 8, 8 * at + 7] = 1.0
    mass = joined @ np.tile(weights, ez)
    gather = np.kron(eye, back.T) @ joined / mass[None, :]
    high, low = halves(gather)
    gather = np.concatenate([high, high, low], axis=0)
    own, rise = [], []
    slope_hats = hats @ derivative
    for f in range(3):
        own_pair, wide_pair = [], []
        for d in range(2):
            hat = slope_hats if f == d else hats
            rows = 8 if d else 5
            plain = np.zeros((rows, 16))
            for e in range(2):
                for a in range(2):
                    plain[e + a + 1, 8 * e : 8 * e + 8] += hat[a]
            shared = plain.copy()
            for a in range(2):
                shared[a, 0] += hat[a, 7]
                shared[3 + a, 15] += hat[a, 0]
            own_pair.append(plain)
            wide_pair.append(shared)
        own_high, own_low = halves(np.kron(*own_pair))
        wide_high, wide_low = halves(step_size * np.kron(*wide_pair))
        own.append(np.concatenate([own_high, own_low, wide_high, wide_high, wide_low], axis=1))
        hat = slope_hats if f == 2 else hats
        up = np.zeros((8 * ez, 128))
        for e in range(ez):
            for a in range(2):
                up[8 * e : 8 * e + 8, e + a] += hat[a]
        high, low = halves(up)
        rise.append(np.concatenate([high, high, low], axis=0))
    fall = np.pad(fall.astype(np.float32), ((0, 0), (0, 80))).astype(jnp.bfloat16)
    blocks = [spread, lift, fall[:, :256], fall[:, 256:], gather]
    blocks += [np.pad(own[f][:, 256 * c : 256 * c + 256].astype(np.float32), ((0, 8), (0, 0))).astype(jnp.bfloat16)
               for f in range(3) for c in range(5)]
    blocks += [np.concatenate(rise[:2], axis=1), np.concatenate([rise[2], rise[2]], axis=1)]
    return np.concatenate(blocks, axis=0)


def first_kernel(
    fields_far, table_far, out_far, near_side, far_side, low_y, high_y, hold,
    fields, table, points, down, out, arrivals, departure,
):
    ends = (0, 1024, 1584, 2736, 4992)
    loads = [pltpu.make_async_copy(fields_far, fields, arrivals.at[0])]
    for at in range(4):
        rows = pl.ds(ends[at], ends[at + 1] - ends[at])
        loads.append(
            pltpu.make_async_copy(table_far.at[rows], table.at[rows], arrivals.at[at + 1])
        )
    for load in loads:
        load.start()
    loads[0].wait()
    nodes = fields[...].astype(f32).reshape(1024, 256).astype(bf16)
    loads[1].wait()
    for at, piece, rows in (
        (0, nodes[:, :128], slice(0, 256)),
        (512, nodes[:, 128:], slice(256, 512)),
        (256, nodes, slice(512, 1024)),
    ):
        points[..., at : at + 256] = jnp.dot(
            jnp.concatenate([piece, piece], axis=1), table[rows], preferred_element_type=f32
        ).reshape(4, 2, 8, 2, 8, 256)
    loads[2].wait()

    def column(ex, carry):
        lift = table[1024:1456]
        fall = jnp.concatenate([table[1456:1520], table[1520:1584][:, :176]], axis=1)
        speeds = []
        slopes = []
        for f in range(4):
            first = points[f, ex, :, 0].reshape(64, 768)
            second = points[f, ex, :, 1].reshape(64, 768)
            sides = []
            for side in range(2):
                lanes = [slice(at, at + 128) for at in range(128 * side, 768, 256)]
                pieces = [first[:, at] for at in lanes] + [second[:, at] for at in lanes]
                high, low = split(jnp.concatenate(pieces, axis=1))
                sides.append(jnp.concatenate([high, high, low, low], axis=0))
            flat = jnp.dot(lift if f < 3 else lift[:288], sides[0], preferred_element_type=f32)
            steep = jnp.dot(lift[288:], sides[1], preferred_element_type=f32)
            if f < 3:
                speeds.append(flat[288:])
            slopes.append((flat[:144], flat[144:288], steep))
        for f in range(4):
            product = sum(speeds[d] * slopes[f][d] for d in range(3))
            high, low = split(product)
            stacked = jnp.concatenate([high, low, high], axis=0)
            fallen = jnp.dot(fall, stacked, preferred_element_type=f32)
            down[f, ex, :, 0] = fallen[:, :384].reshape(8, 8, 384)
            down[f, ex, :, 1] = fallen[:, 384:].reshape(8, 8, 384)
        return carry

    column(0, 0)
    column(1, 0)
    high, low = split(down[...].reshape(1024, 384))
    loads[3].wait()
    stacked = jnp.concatenate([high, low, high], axis=1)
    stores = []
    for pair in range(2):
        part = pl.ds(2 * pair, 2)
        out[part] = jnp.dot(
            stacked[512 * pair : 512 * pair + 512], table[1584:2736], preferred_element_type=f32
        ).reshape(2, 2, 8, 2, 8, 256)
        middle = out[part, 0, 7] + out[part, 1, 0]
        out[part, 0, 7] = middle
        out[part, 1, 0] = middle
        middle = out[part, :, :, 0, 7:8] + out[part, :, :, 1, 0:1]
        out[part, :, :, 0, 7:8] = middle
        out[part, :, :, 1, 0:1] = middle
        stores.append(pltpu.make_async_copy(out.at[part], out_far.at[part], departure.at[pair]))
        stores[pair].start()
    low_y[...] = out[:, :, :, 0, 0].reshape(64, 256)
    high_y[...] = out[:, :, :, 1, 7].reshape(64, 256)
    loads[4].wait()
    total = jnp.zeros((40, 128), f32)
    for f in range(3):
        high, low = split(out[f].reshape(256, 256))
        part = nodes[256 * f : 256 * (f + 1)]
        stacked = jnp.concatenate([part, part, high, low, high], axis=0)
        own = [table[2736 + 48 * c : 2784 + 48 * c] for c in range(5 * f, 5 * f + 5)]
        flat = jnp.dot(jnp.concatenate(own, axis=1), stacked, preferred_element_type=f32)
        high, low = split(flat[:40])
        start, lanes = 3456 + 768 * (f // 2), slice(128 * (f % 2), 128 * (f % 2) + 128)
        total = total + jnp.dot(
            jnp.concatenate([high, low, high], axis=1),
            table[start : start + 768, lanes],
            preferred_element_type=f32,
        )
    hold[...] = total[8:24]
    even = lax.axis_index("core") == 0
    low_face = out[:, 0, 0].reshape(64, 256)
    high_face = out[:, 1, 7].reshape(64, 256)
    far_side[:64] = jnp.where(even, low_face, high_face)
    far_side[64:, :128] = jnp.where(even, total[:8], total[24:32])
    far_side[64:, 128:] = jnp.where(even, 0.0, total[32:])
    chosen = jnp.where(even, high_face, low_face)
    first = jnp.where(even, total[24:32], total[:8])
    second = jnp.where(even, total[32:], 0.0)
    near_side[:64] = chosen
    near_side[64:, :128] = first
    near_side[64:, 128:] = second
    for store in stores:
        store.wait()


def sides(near_side, far_side, axis):
    me = lax.axis_index(axis)
    even = me == 0
    beside = near_side[1 - me]
    beyond = far_side[...]
    return jnp.where(even, beyond, beside), jnp.where(even, beside, beyond)


def second_kernel(
    near_side, far_side, low_y, high_y, hold, sep, near_out, far_out, hold_out, from_low, from_high
):
    from_low[...], from_high[...] = sides(near_side, far_side, "core")
    even = lax.axis_index("pair") == 0
    low_face = low_y[...]
    high_face = high_y[...]
    near_out[:64] = jnp.where(even, high_face, low_face)
    far_out[:64] = jnp.where(even, low_face, high_face)
    for f in range(4):
        for at, source, row in ((16 * f, from_low, 16 * f), (16 * f + 15, from_high, 16 * f)):
            place = slice(at, at + 1)
            low_sum = low_y[place] + source[row : row + 1]
            high_sum = high_y[place] + source[row + 15 : row + 16]
            near_out[place] = jnp.where(even, high_sum, low_sum)
            far_out[place] = jnp.where(even, low_sum, high_sum)
    near = hold[:8] + from_low[64:, :128]
    far = hold[8:] + from_low[64:, 128:] + from_high[64:, :128]
    hold_out[:8] = near
    hold_out[8:] = far
    for target in (near_out, far_out):
        target[64:, :128] = near
        target[64:, 128:] = far


def third_kernel(partial, from_low, from_high, out):
    out[...] = partial[...]
    out[:, 0, 0] = partial[:, 0, 0] + from_low[:64].reshape(4, 2, 8, 256)
    out[:, 1, 7] = partial[:, 1, 7] + from_high[:64].reshape(4, 2, 8, 256)


def right_side(near_side, far_side, hold):
    low_rows, high_rows = sides(near_side.at[:, 64:], far_side.at[64:], "pair")
    rows = []
    for vx in range(2):
        lanes = slice(128 * vx, 128 * vx + 128)
        rows.append(hold[8 * vx + 1 : 8 * vx + 2] + low_rows[3:4, lanes])
        rows.append(
            hold[8 * vx + 2 : 8 * vx + 3] + low_rows[4:5, lanes] + high_rows[0:1, lanes]
        )
    upright = jnp.transpose(jnp.concatenate(rows + rows, axis=0))
    return [upright[:33, v : v + 1] for v in range(4)]


def fourth_kernel(near_side, far_side, hold, sep, sums):
    columns = right_side(near_side, far_side, hold)
    for at in range(8):
        lanes = slice(128 * at, 128 * at + 128)
        total = sum(columns[v] * sep[v // 2, v % 2, :, lanes] for v in range(4))
        sums[0, at : at + 1] = jnp.sum(total, axis=0, keepdims=True)
    sums[1:] = jnp.broadcast_to(sums[0][None], (sums.shape[0] - 1, 8, 128))


def inner_kernel(near_side, far_side, hold, inner, term):
    columns = right_side(near_side, far_side, hold)
    total = sum(columns[v] * inner[v // 2, v % 2] for v in range(4))
    total = jnp.sum(total, axis=0, keepdims=True)
    for v in range(4):
        part = inner[v // 2, v % 2] * total
        term[v // 2, v % 2 : v % 2 + 1] = jnp.sum(part, axis=1)[None]


def fifth_kernel(partial, near_side, far_side, out):
    low_face, high_face = sides(near_side.at[:, :64], far_side.at[:64], "pair")
    out[...] = partial[...]
    out[:, :, :, 0, 0] = partial[:, :, :, 0, 0] + low_face.reshape(4, 2, 8, 256)
    out[:, :, :, 1, 7] = partial[:, :, :, 1, 7] + high_face.reshape(4, 2, 8, 256)


def spread_kernel(parts, copies):
    total = jnp.sum(parts[...], axis=0)
    copies[...] = jnp.broadcast_to(total[None], copies.shape)


def last_kernel(arrived, sep, term, out):
    total = jnp.sum(arrived[...], axis=0)
    for v in range(4):
        part = sum(
            sep[v // 2, v % 2, :, 128 * at : 128 * at + 128] * total[at : at + 1] for at in range(8)
        )
        out[v // 2, v % 2 : v % 2 + 1] = (
            term[v // 2, v % 2 : v % 2 + 1] + jnp.sum(part, axis=1)[None]
        )


def call(kernel, shapes, arrays):
    whole = pl.BlockSpec(memory_space=pltpu.VMEM)
    return pl.pallas_call(
        kernel,
        out_shape=[jax.ShapeDtypeStruct(s, f32) for s in shapes],
        in_specs=[whole] * len(arrays),
        out_specs=[whole] * len(shapes),
        compiler_params=pltpu.CompilerParams(vmem_limit_bytes=16 * 2**20),
    )(*arrays)


def first(fields):
    arrays = [fields, jnp.asarray(constants(fields.shape[5] // 8))]
    shapes = [fields.shape, (72, 256), (72, 256), (64, 256), (64, 256), (16, 128)]
    whole = pl.BlockSpec(memory_space=pltpu.VMEM)
    beyond = pl.BlockSpec(memory_space=pltpu.HBM)
    return pl.pallas_call(
        first_kernel,
        out_shape=[jax.ShapeDtypeStruct(s, f32) for s in shapes],
        in_specs=[beyond, beyond],
        out_specs=[beyond] + [whole] * 5,
        scratch_shapes=[pltpu.VMEM(a.shape, a.dtype) for a in arrays]
        + [
            pltpu.VMEM((4, 2, 8, 2, 8, 768), f32),
            pltpu.VMEM((4, 2, 8, 2, 8, 384), f32),
            pltpu.VMEM(fields.shape, f32),
            pltpu.SemaphoreType.DMA((5,)),
            pltpu.SemaphoreType.DMA((2,)),
        ],
        compiler_params=pltpu.CompilerParams(vmem_limit_bytes=214 * 2**18),
    )(*arrays)


def moved(x, axis, target):
    return lax.ppermute(x, axis, [(i, target(i)) for i in range(lax.axis_size(axis))])


slab = ("high", "low", "x", "core")
cross = ("half", "pair")


def swapped(x, axis):
    count = lax.axis_size(axis)
    return moved(x, axis, lambda i: (i + (1 if i % 2 else count - 1)) % count)


def local(fields, sep_factor, local_factor):
    partial, near_side, far_side, low_y, high_y, hold = first(fields)
    far_side = swapped(far_side, slab)
    near_side = lax.all_gather(near_side, "core")
    near_y, far_y, hold, from_low, from_high = call(
        second_kernel,
        [(72, 256), (72, 256), (16, 128), (72, 256), (72, 256)],
        [near_side, far_side, low_y, high_y, hold, sep_factor],
    )
    far_y = swapped(far_y, cross)
    near_y = lax.all_gather(near_y, "pair")
    partial = call(third_kernel, [fields.shape], [partial, from_low, from_high])[0]
    across = ("x", "pair", "half")
    along = ("low", "core", "high")
    sums = call(
        fourth_kernel,
        [(lax.axis_size(across), 8, 128)],
        [near_y, far_y, hold, sep_factor],
    )[0]
    term = call(inner_kernel, [(2, 2, 33)], [near_y, far_y, hold, local_factor])[0]
    conv_rate = call(fifth_kernel, [fields.shape], [partial, near_y, far_y])[0]
    sums = lax.all_to_all(sums, across, 0, 0)
    sums = call(spread_kernel, [(lax.axis_size(along), 8, 128)], [sums])[0]
    sums = lax.all_to_all(sums, along, 0, 0)
    pressure = call(last_kernel, [(2, 2, 33)], [sums, sep_factor, term])[0]
    return conv_rate, pressure


def solution(mesh):
    fine = Mesh(mesh.devices.reshape(3, 4, 4, 2, 4, 2), slab + cross)
    return jax.shard_map(
        local,
        mesh=fine,
        in_specs=(
            P(None, slab, None, cross, None, None),
            P(slab, cross, None, None),
            P(slab, cross, None, None),
        ),
        out_specs=(P(None, slab, None, cross, None, None), P(slab, cross, None)),
        check_vma=False,
    )
```

```python
import functools

import jax
import jax.numpy as jnp
import numpy as np
from jax import lax
from jax.experimental import pallas as pl
from jax.experimental.pallas import tpu as pltpu
from jax.sharding import Mesh
from jax.sharding import PartitionSpec as P

degree = 7
step_size = 0.25
bf16 = jnp.bfloat16
f32 = jnp.float32


def legendre_values(order, points):
    earlier = points * 0.0 + 1.0
    current = points * 1.0
    for level_index in range(1, order):
        follow = ((2 * level_index + 1) * points * current - level_index * earlier) / (
            level_index + 1
        )
        earlier = current
        current = follow
    return current


def tables():
    gll_nodes = np.array(
        [
            -1.0,
            -0.8717401485096066,
            -0.5917001814331423,
            -0.2092992179024789,
            0.2092992179024789,
            0.5917001814331423,
            0.8717401485096066,
            1.0,
        ]
    )
    at_nodes = legendre_values(degree, gll_nodes)
    weights = 2.0 / (degree * (degree + 1) * at_nodes**2)
    points = degree + 1
    derivative = np.zeros((points, points))
    for target in range(points):
        for source in range(points):
            if target != source:
                derivative[target, source] = at_nodes[target] / (
                    at_nodes[source] * (gll_nodes[target] - gll_nodes[source])
                )
    derivative[0, 0] = -degree * (degree + 1) / 4.0
    derivative[-1, -1] = degree * (degree + 1) / 4.0
    half_nodes = np.array(
        [
            0.1252334085114689,
            0.3678314989981802,
            0.5873179542866175,
            0.7699026741943047,
            0.9041172563704749,
            0.9815606342467192,
        ]
    )
    fine_nodes = np.concatenate([-half_nodes[::-1], half_nodes])
    for newton_step in range(3):
        top_value = legendre_values(12, fine_nodes)
        below_value = legendre_values(11, fine_nodes)
        slope_value = (
            12.0 * (fine_nodes * top_value - below_value) / (fine_nodes * fine_nodes - 1.0)
        )
        fine_nodes = fine_nodes - top_value / slope_value
    top_value = legendre_values(12, fine_nodes)
    below_value = legendre_values(11, fine_nodes)
    slope_value = 12.0 * (fine_nodes * top_value - below_value) / (fine_nodes * fine_nodes - 1.0)
    fine_weights = 2.0 / ((1.0 - fine_nodes * fine_nodes) * slope_value * slope_value)
    interp = np.ones((12, points))
    for source in range(points):
        for target in range(points):
            if target != source:
                interp[:, source] *= (fine_nodes - gll_nodes[target]) / (
                    gll_nodes[source] - gll_nodes[target]
                )
    slope_interp = interp @ derivative
    vertex_hats = np.stack([(1.0 - gll_nodes) / 2.0, (1.0 + gll_nodes) / 2.0]) * weights[None, :]
    return weights, derivative, interp, slope_interp, fine_weights, vertex_hats


def halves(matrix):
    high = matrix.astype(np.float32).astype(jnp.bfloat16)
    low = (matrix - high.astype(np.float64)).astype(np.float32).astype(jnp.bfloat16)
    return high, low


def split(x):
    high = x.astype(bf16)
    return high, (x - high.astype(f32)).astype(bf16)


def constants(ez):
    weights, derivative, interp, slope_interp, fine_weights, hats = tables()
    eye = np.eye(ez)
    flat, steep = np.kron(eye, interp.T), np.kron(eye, slope_interp.T)
    spread = []
    for at, rows in ((0, slice(0, 128)), (2, slice(128, 256)), (1, slice(0, 256))):
        lanes = slice(128 * at, 128 * at + 128)
        spread += halves(np.concatenate([flat[rows, lanes], steep[rows, lanes]], axis=1))
    spread = np.concatenate(spread, axis=0)
    lift = np.concatenate(
        [np.kron(slope_interp, interp), np.kron(interp, slope_interp), np.kron(interp, interp)]
    )
    high, low = halves(lift)
    lift = np.concatenate([high, low, high, low], axis=1)
    across = weights.copy()
    across[0] = across[7] = weights[0] + weights[7]
    back = interp.T * fine_weights[None, :]
    fall = -np.kron(back / across[:, None], back / across[:, None])
    high, low = halves(fall)
    fall = np.concatenate([high, high, low], axis=1)
    joined = np.eye(8 * ez)
    for at in range(ez - 1):
        joined[8 * at + 7, 8 * at + 8] = joined[8 * at + 8, 8 * at + 7] = 1.0
    mass = joined @ np.tile(weights, ez)
    gather = np.kron(eye, back.T) @ joined / mass[None, :]
    high, low = halves(gather)
    gather = np.concatenate([high, high, low], axis=0)
    own, rise = [], []
    slope_hats = hats @ derivative
    for f in range(3):
        own_pair, wide_pair = [], []
        for d in range(2):
            hat = slope_hats if f == d else hats
            rows = 8 if d else 5
            plain = np.zeros((rows, 16))
            for e in range(2):
                for a in range(2):
                    plain[e + a + 1, 8 * e : 8 * e + 8] += hat[a]
            shared = plain.copy()
            for a in range(2):
                shared[a, 0] += hat[a, 7]
                shared[3 + a, 15] += hat[a, 0]
            own_pair.append(plain)
            wide_pair.append(shared)
        own_high, own_low = halves(np.kron(*own_pair))
        wide_high, wide_low = halves(step_size * np.kron(*wide_pair))
        own.append(np.concatenate([own_high, own_low, wide_high, wide_high, wide_low], axis=1))
        hat = slope_hats if f == 2 else hats
        up = np.zeros((8 * ez, 128))
        for e in range(ez):
            for a in range(2):
                up[8 * e : 8 * e + 8, e + a] += hat[a]
        high, low = halves(up)
        rise.append(np.concatenate([high, high, low], axis=0))
    fall = np.pad(fall.astype(np.float32), ((0, 0), (0, 80))).astype(jnp.bfloat16)
    blocks = [spread, lift, fall[:, :256], fall[:, 256:], gather]
    blocks += [np.pad(own[f][:, 256 * c : 256 * c + 256].astype(np.float32), ((0, 8), (0, 0))).astype(jnp.bfloat16)
               for f in range(3) for c in range(5)]
    blocks += [np.concatenate(rise[:2], axis=1), np.concatenate([rise[2], rise[2]], axis=1)]
    return np.concatenate(blocks, axis=0)


def first_kernel(
    fields_far, table_far, out_far, near_side, far_side, low_y, high_y, hold,
    fields, table, points, down, out, arrivals, departure,
):
    ends = (0, 1024, 1584, 2736, 4992)
    loads = [pltpu.make_async_copy(fields_far, fields, arrivals.at[0])]
    for at in range(4):
        rows = pl.ds(ends[at], ends[at + 1] - ends[at])
        loads.append(
            pltpu.make_async_copy(table_far.at[rows], table.at[rows], arrivals.at[at + 1])
        )
    for load in loads:
        load.start()
    loads[0].wait()
    nodes = fields[...].astype(f32).reshape(1024, 256).astype(bf16)
    loads[1].wait()
    for at, piece, rows in (
        (0, nodes[:, :128], slice(0, 256)),
        (512, nodes[:, 128:], slice(256, 512)),
        (256, nodes, slice(512, 1024)),
    ):
        points[..., at : at + 256] = jnp.dot(
            jnp.concatenate([piece, piece], axis=1), table[rows], preferred_element_type=f32
        ).reshape(4, 2, 8, 2, 8, 256)
    loads[2].wait()

    def column(ex, carry):
        lift = table[1024:1456]
        fall = jnp.concatenate([table[1456:1520], table[1520:1584][:, :176]], axis=1)
        speeds = []
        slopes = []
        for f in range(4):
            first = points[f, ex, :, 0].reshape(64, 768)
            second = points[f, ex, :, 1].reshape(64, 768)
            sides = []
            for side in range(2):
                lanes = [slice(at, at + 128) for at in range(128 * side, 768, 256)]
                pieces = [first[:, at] for at in lanes] + [second[:, at] for at in lanes]
                high, low = split(jnp.concatenate(pieces, axis=1))
                sides.append(jnp.concatenate([high, high, low, low], axis=0))
            flat = jnp.dot(lift if f < 3 else lift[:288], sides[0], preferred_element_type=f32)
            steep = jnp.dot(lift[288:], sides[1], preferred_element_type=f32)
            if f < 3:
                speeds.append(flat[288:])
            slopes.append((flat[:144], flat[144:288], steep))
        for f in range(4):
            product = sum(speeds[d] * slopes[f][d] for d in range(3))
            high, low = split(product)
            stacked = jnp.concatenate([high, low, high], axis=0)
            fallen = jnp.dot(fall, stacked, preferred_element_type=f32)
            down[f, ex, :, 0] = fallen[:, :384].reshape(8, 8, 384)
            down[f, ex, :, 1] = fallen[:, 384:].reshape(8, 8, 384)
        return carry

    column(0, 0)
    column(1, 0)
    high, low = split(down[...].reshape(1024, 384))
    loads[3].wait()
    stacked = jnp.concatenate([high, low, high], axis=1)
    stores = []
    for pair in range(2):
        part = pl.ds(2 * pair, 2)
        out[part] = jnp.dot(
            stacked[512 * pair : 512 * pair + 512], table[1584:2736], preferred_element_type=f32
        ).reshape(2, 2, 8, 2, 8, 256)
        middle = out[part, 0, 7] + out[part, 1, 0]
        out[part, 0, 7] = middle
        out[part, 1, 0] = middle
        middle = out[part, :, :, 0, 7:8] + out[part, :, :, 1, 0:1]
        out[part, :, :, 0, 7:8] = middle
        out[part, :, :, 1, 0:1] = middle
        stores.append(pltpu.make_async_copy(out.at[part], out_far.at[part], departure.at[pair]))
        stores[pair].start()
    low_y[...] = out[:, :, :, 0, 0].reshape(64, 256)
    high_y[...] = out[:, :, :, 1, 7].reshape(64, 256)
    loads[4].wait()
    total = jnp.zeros((40, 128), f32)
    for f in range(3):
        high, low = split(out[f].reshape(256, 256))
        part = nodes[256 * f : 256 * (f + 1)]
        stacked = jnp.concatenate([part, part, high, low, high], axis=0)
        own = [table[2736 + 48 * c : 2784 + 48 * c] for c in range(5 * f, 5 * f + 5)]
        flat = jnp.dot(jnp.concatenate(own, axis=1), stacked, preferred_element_type=f32)
        high, low = split(flat[:40])
        start, lanes = 3456 + 768 * (f // 2), slice(128 * (f % 2), 128 * (f % 2) + 128)
        total = total + jnp.dot(
            jnp.concatenate([high, low, high], axis=1),
            table[start : start + 768, lanes],
            preferred_element_type=f32,
        )
    hold[...] = total[8:24]
    even = lax.axis_index("core") == 0
    low_face = out[:, 0, 0].reshape(64, 256)
    high_face = out[:, 1, 7].reshape(64, 256)
    far_side[:64] = jnp.where(even, low_face, high_face)
    far_side[64:, :128] = jnp.where(even, total[:8], total[24:32])
    far_side[64:, 128:] = jnp.where(even, 0.0, total[32:])
    chosen = jnp.where(even, high_face, low_face)
    first = jnp.where(even, total[24:32], total[:8])
    second = jnp.where(even, total[32:], 0.0)
    near_side[:64] = chosen
    near_side[64:, :128] = first
    near_side[64:, 128:] = second
    for store in stores:
        store.wait()


def sides(near_side, far_side, axis):
    me = lax.axis_index(axis)
    even = me == 0
    beside = near_side[1 - me]
    beyond = far_side[...]
    return jnp.where(even, beyond, beside), jnp.where(even, beside, beyond)


def second_kernel(
    near_side, far_side, low_y, high_y, hold, sep, near_out, far_out, hold_out, from_low, from_high
):
    from_low[...], from_high[...] = sides(near_side, far_side, "core")
    even = lax.axis_index("pair") == 0
    low_face = low_y[...]
    high_face = high_y[...]
    near_out[:64] = jnp.where(even, high_face, low_face)
    far_out[:64] = jnp.where(even, low_face, high_face)
    for f in range(4):
        for at, source, row in ((16 * f, from_low, 16 * f), (16 * f + 15, from_high, 16 * f)):
            place = slice(at, at + 1)
            low_sum = low_y[place] + source[row : row + 1]
            high_sum = high_y[place] + source[row + 15 : row + 16]
            near_out[place] = jnp.where(even, high_sum, low_sum)
            far_out[place] = jnp.where(even, low_sum, high_sum)
    near = hold[:8] + from_low[64:, :128]
    far = hold[8:] + from_low[64:, 128:] + from_high[64:, :128]
    hold_out[:8] = near
    hold_out[8:] = far
    for target in (near_out, far_out):
        target[64:, :128] = near
        target[64:, 128:] = far


def third_kernel(partial, from_low, from_high, out):
    out[...] = partial[...]
    out[:, 0, 0] = partial[:, 0, 0] + from_low[:64].reshape(4, 2, 8, 256)
    out[:, 1, 7] = partial[:, 1, 7] + from_high[:64].reshape(4, 2, 8, 256)


def right_side(near_side, far_side, hold):
    low_rows, high_rows = sides(near_side.at[:, 64:], far_side.at[64:], "pair")
    rows = []
    for vx in range(2):
        lanes = slice(128 * vx, 128 * vx + 128)
        rows.append(hold[8 * vx + 1 : 8 * vx + 2] + low_rows[3:4, lanes])
        rows.append(
            hold[8 * vx + 2 : 8 * vx + 3] + low_rows[4:5, lanes] + high_rows[0:1, lanes]
        )
    upright = jnp.transpose(jnp.concatenate(rows + rows, axis=0))
    return [upright[:33, v : v + 1] for v in range(4)]


def fourth_kernel(near_side, far_side, hold, sep, sums):
    columns = right_side(near_side, far_side, hold)
    for at in range(8):
        lanes = slice(128 * at, 128 * at + 128)
        total = sum(columns[v] * sep[v // 2, v % 2, :, lanes] for v in range(4))
        sums[0, at : at + 1] = jnp.sum(total, axis=0, keepdims=True)
    sums[1:] = jnp.broadcast_to(sums[0][None], (sums.shape[0] - 1, 8, 128))


def inner_kernel(near_side, far_side, hold, inner, term):
    columns = right_side(near_side, far_side, hold)
    total = sum(columns[v] * inner[v // 2, v % 2] for v in range(4))
    total = jnp.sum(total, axis=0, keepdims=True)
    for v in range(4):
        part = inner[v // 2, v % 2] * total
        term[v // 2, v % 2 : v % 2 + 1] = jnp.sum(part, axis=1)[None]


def fifth_kernel(partial, near_side, far_side, out):
    low_face, high_face = sides(near_side.at[:, :64], far_side.at[:64], "pair")
    out[...] = partial[...]
    out[:, :, :, 0, 0] = partial[:, :, :, 0, 0] + low_face.reshape(4, 2, 8, 256)
    out[:, :, :, 1, 7] = partial[:, :, :, 1, 7] + high_face.reshape(4, 2, 8, 256)


def spread_kernel(parts, copies):
    total = jnp.sum(parts[...], axis=0)
    copies[...] = jnp.broadcast_to(total[None], copies.shape)


def last_kernel(arrived, sep, term, out):
    total = jnp.sum(arrived[...], axis=0)
    for v in range(4):
        part = sum(
            sep[v // 2, v % 2, :, 128 * at : 128 * at + 128] * total[at : at + 1] for at in range(8)
        )
        out[v // 2, v % 2 : v % 2 + 1] = (
            term[v // 2, v % 2 : v % 2 + 1] + jnp.sum(part, axis=1)[None]
        )


def call(kernel, shapes, arrays):
    whole = pl.BlockSpec(memory_space=pltpu.VMEM)
    return pl.pallas_call(
        kernel,
        out_shape=[jax.ShapeDtypeStruct(s, f32) for s in shapes],
        in_specs=[whole] * len(arrays),
        out_specs=[whole] * len(shapes),
        compiler_params=pltpu.CompilerParams(vmem_limit_bytes=16 * 2**20),
    )(*arrays)


def first(fields):
    arrays = [fields, jnp.asarray(constants(fields.shape[5] // 8))]
    shapes = [fields.shape, (72, 256), (72, 256), (64, 256), (64, 256), (16, 128)]
    whole = pl.BlockSpec(memory_space=pltpu.VMEM)
    beyond = pl.BlockSpec(memory_space=pltpu.HBM)
    return pl.pallas_call(
        first_kernel,
        out_shape=[jax.ShapeDtypeStruct(s, f32) for s in shapes],
        in_specs=[beyond, beyond],
        out_specs=[beyond] + [whole] * 5,
        scratch_shapes=[pltpu.VMEM(a.shape, a.dtype) for a in arrays]
        + [
            pltpu.VMEM((4, 2, 8, 2, 8, 768), f32),
            pltpu.VMEM((4, 2, 8, 2, 8, 384), f32),
            pltpu.VMEM(fields.shape, f32),
            pltpu.SemaphoreType.DMA((5,)),
            pltpu.SemaphoreType.DMA((2,)),
        ],
        compiler_params=pltpu.CompilerParams(vmem_limit_bytes=214 * 2**18),
    )(*arrays)


def moved(x, axis, target):
    return lax.ppermute(x, axis, [(i, target(i)) for i in range(lax.axis_size(axis))])


slab = ("high", "low", "x", "core")
cross = ("half", "pair")


def swapped(x, axis):
    count = lax.axis_size(axis)
    return moved(x, axis, lambda i: (i + (1 if i % 2 else count - 1)) % count)


def local(fields, sep_factor, local_factor):
    partial, near_side, far_side, low_y, high_y, hold = first(fields)
    far_side, sep_factor, local_factor = lax.optimization_barrier(
        (far_side, sep_factor, local_factor)
    )
    far_side = swapped(far_side, slab)
    near_side = lax.all_gather(near_side, "core")
    near_y, far_y, hold, from_low, from_high = call(
        second_kernel,
        [(72, 256), (72, 256), (16, 128), (72, 256), (72, 256)],
        [near_side, far_side, low_y, high_y, hold, sep_factor],
    )
    far_y = swapped(far_y, cross)
    near_y = lax.all_gather(near_y, "pair")
    partial = call(third_kernel, [fields.shape], [partial, from_low, from_high])[0]
    across = ("x", "pair", "half")
    along = ("low", "core", "high")
    sums = call(
        fourth_kernel,
        [(lax.axis_size(across), 8, 128)],
        [near_y, far_y, hold, sep_factor],
    )[0]
    term = call(inner_kernel, [(2, 2, 33)], [near_y, far_y, hold, local_factor])[0]
    conv_rate = call(fifth_kernel, [fields.shape], [partial, near_y, far_y])[0]
    sums = lax.all_to_all(sums, across, 0, 0)
    sums = call(spread_kernel, [(lax.axis_size(along), 8, 128)], [sums])[0]
    sums = lax.all_to_all(sums, along, 0, 0)
    pressure = call(last_kernel, [(2, 2, 33)], [sums, sep_factor, term])[0]
    return conv_rate, pressure


def solution(mesh):
    fine = Mesh(mesh.devices.reshape(3, 4, 4, 2, 4, 2), slab + cross)
    return jax.shard_map(
        local,
        mesh=fine,
        in_specs=(
            P(None, slab, None, cross, None, None),
            P(slab, cross, None, None),
            P(slab, cross, None, None),
        ),
        out_specs=(P(None, slab, None, cross, None, None), P(slab, cross, None)),
        check_vma=False,
    )
```
